32 devices in a mesh: row: 8 (over z, x), col: 4 (over y, core).
Axes of the slice: x: 2, y: 2, z: 4, core: 2. Of those that a mesh axis runs over, the one named last changes fastest.
Arguments:
- features: bfloat16 [96, 128, 1024], P(None, 'row', 'col'), may hold values from -6 to 6
- teacher: bfloat16 [1536, 128, 1024], P(None, 'row', 'col'), may hold values from -6 to 6
- conv_in: bfloat16 [9, 96, 96], replicated, may hold values from -0.21875 to 0.21875
- conv_out: bfloat16 [9, 96, 96], replicated, may hold values from -0.21875 to 0.21875
- projector: bfloat16 [96, 1536], replicated, may hold values from -0.625 to 0.625
Outputs:
- grad_conv_in: float32 [9, 96, 96], replicated
- grad_conv_out: float32 [9, 96, 96], replicated
- grad_projector: float32 [96, 1536], replicated
The draws below stay inside these ranges and needn't reach their ends.
All inputs are finite; a program needn't handle non-finite values.
Results may differ from the reference program's by a relative error of at most 0.0003.
Values may be sent and summed in bfloat16 or wider, within the bound.
No kernel may reach another device: no remote copies, remote signals or barrier semaphores. Data moves between devices by JAX's collectives and lax.ppermute only.
A program may use at most 128 MiB of HBM per device.

```python
import jax
import jax.numpy as jnp
from jax import lax

C = 96
E = 1536
TH = 16
IMG_H = 128
IMG_W = 1024


def block_scale(key, extent, shards, low, high):
    loudness = 1.0
    for position, parts in shards:
        draws = jax.random.uniform(jax.random.fold_in(jax.random.fold_in(key, 6), position), (parts,), jnp.float32, low / len(shards), high / len(shards))
        loudness = loudness * jnp.repeat(jnp.exp(draws), extent[position] // parts).reshape((-1,) + (1,) * (len(extent) - 1 - position))
    return loudness


def scatter_about(rng, shape, scale, limit, cuts=(), held_as=jnp.bfloat16):
    drawn = scale * jax.random.normal(rng, shape, jnp.float32)
    if cuts:
        drawn = drawn * block_scale(rng, shape, cuts, -0.22, 0.18)
    return jnp.clip(drawn, -limit, limit).astype(held_as)


def setup_inputs(seed: int = 0) -> dict:
    keys = jax.random.split(jax.random.key(seed), 6)
    features = scatter_about(keys[0], (C, IMG_H, IMG_W), 1.0, 6.0, ((1, 8), (2, 4)))
    teacher = scatter_about(keys[1], (E, IMG_H, IMG_W), 1.0, 6.0, ((1, 8), (2, 4)))
    conv_in = scatter_about(keys[2], (9, C, C), (9 * C) ** -0.5, 0.21875)
    conv_out = scatter_about(keys[3], (9, C, C), (9 * C) ** -0.5, 0.21875)
    projector = scatter_about(keys[4], (C, E), C ** -0.5, 0.625)
    return dict(features=features, teacher=teacher, conv_in=conv_in, conv_out=conv_out, projector=projector)


def gelu_grad(value):
    cdf = 0.5 * (1.0 + jax.scipy.special.erf(value * 0.7071067811865476))
    dens = jnp.exp(-0.5 * value * value) * 0.3989422804014327
    return cdf + value * dens

def padded_field(field):
    return jnp.pad(field.astype(jnp.float32), ((0, 0), (1, 1), (1, 1)))

def conv_full(padded, kernel):
    total = jnp.zeros((kernel.shape[2], IMG_H, IMG_W), jnp.float32)
    for tap in range(9):
        shift_a, shift_b = (tap // 3, tap % 3)
        window = padded[:, shift_a:shift_a + IMG_H, shift_b:shift_b + IMG_W]
        total = total + jnp.einsum('co,chw->ohw', kernel[tap].astype(jnp.float32), window)
    return total

def reference(features, teacher, conv_in, conv_out, projector):
    xpad = padded_field(features)
    pre = conv_full(xpad, conv_in)
    hidden = jax.nn.gelu(pre, approximate=False).astype(jnp.bfloat16)
    gpad = padded_field(hidden)
    student = (features.astype(jnp.float32) + conv_full(gpad, conv_out)).astype(jnp.bfloat16)
    npix = IMG_H * IMG_W
    proj_f = projector.astype(jnp.float32)
    blocks = IMG_H // TH

    def one_block(carry, index):
        start = (index * TH).astype(jnp.int32)
        stud = lax.dynamic_slice_in_dim(student, start, TH, 1).astype(jnp.float32)
        teach = lax.dynamic_slice_in_dim(teacher, start, TH, 1).astype(jnp.float32)
        pred = jnp.einsum('ce,chw->ehw', proj_f, stud)
        dpred = ((pred - teach) / npix).astype(jnp.bfloat16).astype(jnp.float32)
        carry = carry + jnp.einsum('chw,ehw->ce', stud, dpred)
        dstud = jnp.einsum('ce,ehw->chw', proj_f, dpred).astype(jnp.bfloat16)
        return (carry, dstud)
    grad_projector, pieces = lax.scan(one_block, jnp.zeros((C, E), jnp.float32), jnp.arange(blocks, dtype=jnp.int32))
    dstudent = jnp.transpose(pieces, (1, 0, 2, 3)).reshape(C, IMG_H, IMG_W)
    spad = padded_field(dstudent)
    dhidden = jnp.zeros((C, IMG_H, IMG_W), jnp.float32)
    for tap in range(9):
        shift_a, shift_b = (tap // 3, tap % 3)
        window = spad[:, 2 - shift_a:2 - shift_a + IMG_H, 2 - shift_b:2 - shift_b + IMG_W]
        dhidden = dhidden + jnp.einsum('co,ohw->chw', conv_out[tap].astype(jnp.float32), window)
    dpre = (dhidden * gelu_grad(pre)).astype(jnp.bfloat16).astype(jnp.float32)
    dstud_f = dstudent.astype(jnp.float32)
    grad_out_list = []
    grad_in_list = []
    for tap in range(9):
        shift_a, shift_b = (tap // 3, tap % 3)
        gwin = gpad[:, shift_a:shift_a + IMG_H, shift_b:shift_b + IMG_W]
        xwin = xpad[:, shift_a:shift_a + IMG_H, shift_b:shift_b + IMG_W]
        grad_out_list.append(jnp.einsum('chw,ohw->co', gwin, dstud_f))
        grad_in_list.append(jnp.einsum('chw,ohw->co', xwin, dpre))
    return (jnp.stack(grad_in_list), jnp.stack(grad_out_list), grad_projector)
```

```python
import jax
import jax.numpy as jnp
from jax import lax
from jax.experimental import pallas as pl
from jax.experimental.pallas import tpu as pltpu
from jax.sharding import PartitionSpec as P

F32 = jnp.float32
BF16 = jnp.bfloat16
PITCH = 5


def dot(a, b):
    return jnp.dot(a, b, preferred_element_type=F32)


def dot_nt(a, b):
    return lax.dot_general(a, b, (((1,), (1,)), ((), ())), preferred_element_type=F32)


def split(v):
    hi = v.astype(BF16)
    return hi, (v - hi.astype(F32)).astype(BF16)


def lanes_of(shape):
    return lax.broadcasted_iota(jnp.int32, shape, 1)


def roll(v, by):
    by = by % v.shape[1]
    return v if by == 0 else pltpu.roll(v, by, 1)


def teach_kernel(x_ref, p_ref, t_ref, x2_ref, pt_ref, tr_ref, g_ref, up_ref, dn_ref, buf, sem):
    chans, height, width = x_ref.shape
    ends = t_ref.shape[0]
    parts = sem.shape[0]
    step = ends // parts
    copies = [
        pltpu.make_async_copy(
            t_ref.at[pl.ds(k * step, step)], buf.at[pl.ds(k * step, step)], sem.at[k]
        )
        for k in range(parts)
    ]
    for c in copies:
        c.start()
    rows = jnp.swapaxes(x_ref[...], 0, 1)
    for h in range(height):
        x2_ref[:, h * width : (h + 1) * width] = rows[h]
    proj = p_ref[...]
    hi, lo = split(dot_nt(proj, proj))
    g_ref[:, :chans] = hi
    g_ref[:, chans:] = lo
    for k in range(parts):
        copies[k].wait()
        rows = jnp.swapaxes(buf[k * step : (k + 1) * step], 0, 1)
        for h in range(height):
            tr_ref[k * step : (k + 1) * step, h * width : (h + 1) * width] = rows[h]
        d = dot(p_ref[:, k * step : (k + 1) * step], tr_ref[k * step : (k + 1) * step, :])
        if k == 0:
            pt_ref[...] = d
        else:
            pt_ref[...] += d
    for ref, row, xrow in ((up_ref, 0, 0), (dn_ref, height - 1, height - 3)):
        ref[:, : 3 * width] = x2_ref[:, xrow * width : (xrow + 3) * width]
        hi, lo = split(pt_ref[:, row * width : (row + 1) * width])
        ref[:, 3 * width : 4 * width] = hi
        ref[:, 4 * width :] = lo


def strip_kernel(x2_ref, pt_ref, top_ref, bot_ref, ml_ref, mr_ref):
    width = top_ref.shape[1] // 5
    height = x2_ref.shape[1] // width
    lane = lanes_of((x2_ref.shape[0], 128))
    left = jnp.zeros((x2_ref.shape[0], 128), F32)
    right = left
    for r in range(height + 6):
        if r < 3:
            ref, base = top_ref, r * width
        elif r < height + 3:
            ref, base = x2_ref, (r - 3) * width
        else:
            ref, base = bot_ref, (r - height - 3) * width
        first = ref[:, base : base + 128].astype(F32)
        last = ref[:, base + width - 128 : base + width].astype(F32)
        at = r * PITCH
        left = jnp.where((lane >= at + 2) & (lane < at + 5), roll(first, at + 2), left)
        right = jnp.where((lane >= at) & (lane < at + 3), roll(last, at - 125), right)
    ml_ref[:, :128] = left.astype(BF16)
    mr_ref[:, :128] = right.astype(BF16)
    left = jnp.zeros((x2_ref.shape[0], 128), F32)
    right = left
    for r in range(height + 2):
        if 1 <= r <= height:
            base = (r - 1) * width
            first = pt_ref[:, base : base + 128]
            last = pt_ref[:, base + width - 128 : base + width]
        else:
            ref = top_ref if r == 0 else bot_ref
            a, b = 3 * width, 4 * width
            first = ref[:, a : a + 128].astype(F32) + ref[:, b : b + 128].astype(F32)
            last = ref[:, b - 128 : b].astype(F32) + ref[:, b + width - 128 :].astype(F32)
        at = r * PITCH
        left = jnp.where(lane == at, roll(first, at), left)
        right = jnp.where(lane == at, roll(last, at - 127), right)
    for ref, v in ((ml_ref, left), (mr_ref, right)):
        hi = v.astype(BF16).astype(F32)
        ref[:, 128:] = (hi + roll(v - hi, 1)).astype(BF16)


def gelu_parts(pre):
    cdf = 0.5 * (1.0 + lax.erf(pre * 0.7071067811865476))
    return pre * cdf, cdf


def main_kernel(
    flags, x2_ref, top_ref, bot_ref, ls_ref, rs_ref, ml_ref, mr_ref, pt_ref, tr_ref, g_ref,
    kin_ref, kout_ref, kback_ref, proj_ref, out_ref,
    x3, h3, d3, grad, s2, dpre2, inv_npix=1.0,
):
    chans = x2_ref.shape[0]
    width = top_ref.shape[1] // 5
    height = x2_ref.shape[1] // width
    has_up, has_dn = flags[0].astype(F32), flags[1].astype(F32)
    has_l, has_r = flags[2].astype(F32), flags[3].astype(F32)
    lane = lanes_of((chans, 128))
    kin, kout, kback = kin_ref[...], kout_ref[...], kback_ref[...]
    gram = g_ref[...]

    def taps(v):
        return jnp.concatenate(
            [roll(v, -(a * PITCH + b)) for a in range(3) for b in range(3)], 0
        ).astype(BF16)

    col = lax.rem(lane, PITCH)
    rowi = lax.div(lane, PITCH)
    halo_l = ls_ref[:, :128].astype(F32)
    halo_r = rs_ref[:, :128].astype(F32)
    strip = jnp.concatenate(
        [
            jnp.where(col < 3, halo_l, roll(ml_ref[:, :128].astype(F32), 1)),
            jnp.where(col >= 2, halo_r, roll(mr_ref[:, :128].astype(F32), -1)),
        ],
        1,
    )
    lane2 = lanes_of((1, 128))
    col1 = lax.rem(lane2, PITCH)
    row1 = lax.div(lane2, PITCH)

    def row_mask(rim):
        inside = jnp.where(row1 < rim, has_up, 1.0)
        return jnp.where(row1 >= height + rim, has_dn, inside)

    hid, _ = gelu_parts(dot(kin, taps(strip)))
    mask = row_mask(2)
    mask = jnp.concatenate(
        [mask * jnp.where(col1 < 2, has_l, 1.0), mask * jnp.where(col1 >= 1, has_r, 1.0)], 1
    )
    hid = (hid * mask).astype(BF16).astype(F32)
    stud = (roll(strip, -(2 * PITCH + 2)) + dot(kout, taps(hid))).astype(BF16)
    halves = jnp.concatenate([ls_ref[:, 128:].astype(F32), rs_ref[:, 128:].astype(F32)], 1)
    pts = halves + roll(halves, -1)
    ds_strip = (dot(gram, jnp.concatenate([stud, stud], 0)) - pts) * inv_npix
    mask = row_mask(1)
    ds_strip = ds_strip * jnp.concatenate([mask * has_l, mask * has_r], 1)
    ds_strip = ds_strip.astype(BF16).astype(F32)

    def put(dst, r, seg, left, at_l, right, at_r):
        lo, hi = r * width, (r + 1) * width
        seg32 = seg.astype(F32)
        ahead = roll(seg32, 1)
        first = jnp.where(lane == 0, roll(left, -at_l), ahead[:, :128])
        dst[0:chans, lo : lo + 128] = first.astype(BF16)
        dst[0:chans, lo + 128 : hi] = ahead[:, 128:].astype(BF16)
        dst[chans : 2 * chans, lo:hi] = seg
        back = roll(seg32, -1)
        last = jnp.where(lane == 127, roll(right, 127 - at_r), back[:, width - 128 :])
        dst[2 * chans :, lo : hi - 128] = back[:, : width - 128].astype(BF16)
        dst[2 * chans :, hi - 128 : hi] = last.astype(BF16)

    def rows3(src, r):
        return jnp.concatenate(
            [src[:, (r + a) * width : (r + a + 1) * width] for a in range(3)], 0
        )

    for r in range(height + 6):
        if r < 3:
            seg = top_ref[:, r * width : (r + 1) * width]
        elif r < height + 3:
            seg = x2_ref[:, (r - 3) * width : (r - 2) * width]
        else:
            seg = bot_ref[:, (r - height - 3) * width : (r - height - 2) * width]
        put(x3, r, seg, halo_l, r * PITCH + 2, halo_r, r * PITCH + 2)

    for r in range(height + 4):
        pre = dot(kin, rows3(x3, r))
        hid_r, cdf = gelu_parts(pre)
        if r < 2:
            hid_r = hid_r * has_up
        elif r >= height + 2:
            hid_r = hid_r * has_dn
        else:
            dens = jnp.exp(-0.5 * pre * pre) * 0.3989422804014327
            grad[:, (r - 2) * width : (r - 1) * width] = cdf + pre * dens
        at = r * PITCH + 1
        put(h3, r, hid_r.astype(BF16), hid[:, :128], at, hid[:, 128:], at)

    for r in range(height + 2):
        seg = x3[chans : 2 * chans, (r + 2) * width : (r + 3) * width]
        stud = (seg.astype(F32) + dot(kout, rows3(h3, r))).astype(BF16)
        if r == 0:
            pt = top_ref[:, 3 * width : 4 * width].astype(F32) + top_ref[:, 4 * width :].astype(F32)
        elif r == height + 1:
            pt = bot_ref[:, 3 * width : 4 * width].astype(F32) + bot_ref[:, 4 * width :].astype(F32)
        else:
            pt = pt_ref[:, (r - 1) * width : r * width]
            s2[:, (r - 1) * width : r * width] = stud
        ds = (dot(gram, jnp.concatenate([stud, stud], 0)) - pt) * inv_npix
        if r == 0:
            ds = ds * has_up
        elif r == height + 1:
            ds = ds * has_dn
        at = r * PITCH
        put(d3, r, ds.astype(BF16), ds_strip[:, :128], at, ds_strip[:, 128:], at)

    for r in range(height):
        span = slice(r * width, (r + 1) * width)
        dpre2[:, span] = (dot(kback, rows3(d3, r)) * grad[:, span]).astype(BF16)

    pixels = height * width
    per = 3 * chans
    offset = pl.cdiv(3 * per, 128) * 128
    for a in range(3):
        base = (a + 2) * width
        out_ref[:, a * per : (a + 1) * per] = dot_nt(dpre2[...], x3[:, base : base + pixels])
        base = (a + 1) * width
        out_ref[:, offset + a * per : offset + (a + 1) * per] = dot_nt(
            d3[chans : 2 * chans, width : width + pixels], h3[:, base : base + pixels]
        )
    out_ref[:, 3 * per : offset] = jnp.zeros((chans, offset - 3 * per), F32)
    out_ref[:, offset + 3 * per : 2 * offset] = jnp.zeros((chans, offset - 3 * per), F32)
    stud = s2[...]
    hi, lo = split(dot_nt(stud, stud))
    proj = proj_ref[...]
    gp = dot(jnp.concatenate([hi, lo], 1), jnp.concatenate([proj, proj], 0))
    out_ref[:, 2 * offset :] = (gp - dot_nt(stud, tr_ref[...])) * inv_npix


def unpack_kernel(v_ref, gin_ref, gout_ref, gproj_ref):
    chans = v_ref.shape[0]
    offset = pl.cdiv(9 * chans, 128) * 128
    for t in range(9):
        gin_ref[t] = v_ref[:, t * chans : (t + 1) * chans].T
        at = offset + t * chans
        gout_ref[t] = v_ref[:, at : at + chans].T
    gproj_ref[...] = v_ref[:, 2 * offset :]


VMEM = pl.BlockSpec(memory_space=pltpu.VMEM)
PARAMS = pltpu.CompilerParams(vmem_limit_bytes=44 << 20)


def swap(v, axis, bit):
    return lax.ppermute(v, axis, [(i, i ^ bit) for i in range(lax.axis_size(axis))])


def bits_of(axis):
    return [1 << k for k in range(lax.axis_size(axis).bit_length() - 1)]


def sum_all(v):
    col, row = bits_of("col"), bits_of("row")
    halved = [("col", col[0], 0), ("col", col[1], 0), ("row", row[0], 1)]
    rest = [("col", b) for b in col[2:]] + [("row", b) for b in row[1:]]
    for axis, bit, dim in halved:
        mine = (lax.axis_index(axis) & bit) // bit
        half = v.shape[dim] // 2
        give = lax.dynamic_slice_in_dim(v, (1 - mine) * half, half, dim)
        keep = lax.dynamic_slice_in_dim(v, mine * half, half, dim)
        v = keep + swap(give, axis, bit)
    for axis, bit in rest:
        v = v + swap(v, axis, bit)
    for axis, bit, dim in halved[::-1]:
        got = swap(v, axis, bit)
        upper = (lax.axis_index(axis) & bit) != 0
        v = jnp.concatenate([jnp.where(upper, got, v), jnp.where(upper, v, got)], dim)
    return v


def shift(v, axis, by):
    n = lax.axis_size(axis)
    return lax.ppermute(v, axis, [(i, i + by) for i in range(n) if 0 <= i + by < n])


def shards(features, teacher, conv_in, conv_out, projector):
    chans, height, width = features.shape
    ends = teacher.shape[0]
    pixels = height * width
    kin = jnp.transpose(conv_in, (2, 0, 1)).reshape(chans, 9 * chans)
    kout = jnp.transpose(conv_out, (2, 0, 1)).reshape(chans, 9 * chans)
    kback = jnp.transpose(conv_out[::-1], (1, 0, 2)).reshape(chans, 9 * chans)
    parts = 6
    x2, pt, tr, gram, up, dn = pl.pallas_call(
        teach_kernel,
        in_specs=[VMEM, VMEM, pl.BlockSpec(memory_space=pl.ANY)],
        out_specs=[VMEM] * 6,
        out_shape=[
            jax.ShapeDtypeStruct((chans, pixels), BF16),
            jax.ShapeDtypeStruct((chans, pixels), F32),
            pltpu.VMEM((ends, pixels), BF16),
            jax.ShapeDtypeStruct((chans, 2 * chans), BF16),
            jax.ShapeDtypeStruct((chans, 5 * width), BF16),
            jax.ShapeDtypeStruct((chans, 5 * width), BF16),
        ],
        scratch_shapes=[
            pltpu.VMEM((ends, height, width), BF16),
            pltpu.SemaphoreType.DMA((parts,)),
        ],
        compiler_params=PARAMS,
        name="teach",
    )(features, projector, teacher)
    bot = shift(up, "row", -1)
    top = shift(dn, "row", 1)
    ml, mr = pl.pallas_call(
        strip_kernel,
        in_specs=[VMEM] * 4,
        out_specs=[VMEM] * 2,
        out_shape=[jax.ShapeDtypeStruct((chans, 256), BF16)] * 2,
        compiler_params=PARAMS,
        name="strips",
    )(x2, pt, top, bot)
    rs = shift(ml, "col", -1)
    ls = shift(mr, "col", 1)
    row, col = lax.axis_index("row"), lax.axis_index("col")
    flags = jnp.stack(
        [row > 0, row < lax.axis_size("row") - 1, col > 0, col < lax.axis_size("col") - 1]
    ).astype(jnp.int32)
    npix = pixels * lax.axis_size("row") * lax.axis_size("col")
    offset = -(-9 * chans // 128) * 128

    def body(*refs):
        main_kernel(*refs, inv_npix=1.0 / npix)

    v = pl.pallas_call(
        body,
        in_specs=[pl.BlockSpec(memory_space=pltpu.SMEM)] + [VMEM] * 14,
        out_specs=VMEM,
        out_shape=jax.ShapeDtypeStruct((chans, 2 * offset + ends), F32),
        scratch_shapes=[
            pltpu.VMEM((3 * chans, (height + 6) * width), BF16),
            pltpu.VMEM((3 * chans, (height + 4) * width), BF16),
            pltpu.VMEM((3 * chans, (height + 2) * width), BF16),
            pltpu.VMEM((chans, pixels), F32),
            pltpu.VMEM((chans, pixels), BF16),
            pltpu.VMEM((chans, pixels), BF16),
        ],
        compiler_params=PARAMS,
        name="block",
    )(flags, x2, top, bot, ls, rs, ml, mr, pt, tr, gram, kin, kout, kback, projector)
    v = sum_all(v)
    return pl.pallas_call(
        unpack_kernel,
        in_specs=[VMEM],
        out_specs=[VMEM] * 3,
        out_shape=[
            jax.ShapeDtypeStruct((9, chans, chans), F32),
            jax.ShapeDtypeStruct((9, chans, chans), F32),
            jax.ShapeDtypeStruct((chans, ends), F32),
        ],
        compiler_params=PARAMS,
        name="unpack",
    )(v)


def solution(mesh):
    in_specs = (P(None, "row", "col"), P(None, "row", "col"), P(), P(), P())
    out_specs = (P(), P(), P())
    return jax.shard_map(shards, mesh=mesh, in_specs=in_specs, out_specs=out_specs, check_vma=False)
```

```python
import functools

import jax
import jax.numpy as jnp
from jax import lax
from jax.experimental import pallas as pl
from jax.experimental.pallas import tpu as pltpu
from jax.sharding import PartitionSpec as P

F32 = jnp.float32
BF16 = jnp.bfloat16
PITCH = 5


def dot(a, b):
    return jnp.dot(a, b, preferred_element_type=F32)


def dot_nt(a, b):
    return lax.dot_general(a, b, (((1,), (1,)), ((), ())), preferred_element_type=F32)


def split(v):
    hi = v.astype(BF16)
    return hi, (v - hi.astype(F32)).astype(BF16)


def lanes_of(shape):
    return lax.broadcasted_iota(jnp.int32, shape, 1)


def roll(v, by):
    by = by % v.shape[1]
    return v if by == 0 else pltpu.roll(v, by, 1)


def strip_rows(left, right, first, last, at, lane):
    left = jnp.where((lane >= at + 2) & (lane < at + 5), roll(first, at + 2), left)
    right = jnp.where((lane >= at) & (lane < at + 3), roll(last, at - 125), right)
    return left, right


def strip_point(left, right, first, last, at, lane):
    left = jnp.where(lane == at, roll(first, at), left)
    right = jnp.where(lane == at, roll(last, at - 127), right)
    return left, right


def teach_kernel(
    x_ref, p_ref, cin_ref, cout_ref, t_ref,
    x2_ref, pt_ref, g_ref, up_ref, dn_ref, own_ref, k_ref, buf, tr, sem,
):
    chans, height, width = x_ref.shape
    ends = t_ref.shape[0]
    parts = sem.shape[0]
    step = ends // parts
    copies = [
        pltpu.make_async_copy(
            t_ref.at[pl.ds(k * step, step)], buf.at[pl.ds(k * step, step)], sem.at[k]
        )
        for k in range(parts)
    ]
    for c in copies:
        c.start()
    rows = jnp.swapaxes(x_ref[...], 0, 1)
    for h in range(height):
        x2_ref[:, h * width : (h + 1) * width] = rows[h]
    proj = p_ref[...]
    hi, lo = split(dot_nt(proj, proj))
    g_ref[:, :chans] = hi
    g_ref[:, chans:] = lo
    k_ref[0] = jnp.concatenate([cin_ref[t].T for t in range(9)], 1)
    k_ref[1] = jnp.concatenate([cout_ref[t].T for t in range(9)], 1)
    k_ref[2] = jnp.concatenate([cout_ref[8 - t] for t in range(9)], 1)
    lane = lanes_of((chans, 128))
    left = right = jnp.zeros((chans, 128), F32)
    for h in range(height):
        first = x2_ref[:, h * width : h * width + 128].astype(F32)
        last = x2_ref[:, (h + 1) * width - 128 : (h + 1) * width].astype(F32)
        left, right = strip_rows(left, right, first, last, (h + 3) * PITCH, lane)
    own_ref[0] = left
    own_ref[1] = right
    for k in range(parts):
        copies[k].wait()
        rows = jnp.swapaxes(buf[k * step : (k + 1) * step], 0, 1)
        for h in range(height):
            tr[k % 2, :, h * width : (h + 1) * width] = rows[h]
        d = dot(p_ref[:, k * step : (k + 1) * step], tr[k % 2])
        if k == 0:
            pt_ref[...] = d
        else:
            pt_ref[...] += d
    left = right = jnp.zeros((chans, 128), F32)
    for h in range(height):
        first = pt_ref[:, h * width : h * width + 128]
        last = pt_ref[:, (h + 1) * width - 128 : (h + 1) * width]
        left, right = strip_point(left, right, first, last, (h + 1) * PITCH, lane)
    own_ref[2] = left
    own_ref[3] = right
    for ref, row, xrow in ((up_ref, 0, 0), (dn_ref, height - 1, height - 3)):
        ref[:, : 3 * width] = x2_ref[:, xrow * width : (xrow + 3) * width]
        hi, lo = split(pt_ref[:, row * width : (row + 1) * width])
        ref[:, 3 * width : 4 * width] = hi
        ref[:, 4 * width :] = lo


def strip_kernel(own_ref, top_ref, bot_ref, ml_ref, mr_ref, *, height):
    chans = top_ref.shape[0]
    width = top_ref.shape[1] // 5
    lane = lanes_of((chans, 128))
    left, right = own_ref[0], own_ref[1]
    for r in range(3):
        for ref, at in ((top_ref, r * PITCH), (bot_ref, (r + height + 3) * PITCH)):
            first = ref[:, r * width : r * width + 128].astype(F32)
            last = ref[:, (r + 1) * width - 128 : (r + 1) * width].astype(F32)
            left, right = strip_rows(left, right, first, last, at, lane)
    ml_ref[:, :128] = left.astype(BF16)
    mr_ref[:, :128] = right.astype(BF16)
    left, right = own_ref[2], own_ref[3]
    a, b = 3 * width, 4 * width
    for ref, at in ((top_ref, 0), (bot_ref, (height + 1) * PITCH)):
        first = ref[:, a : a + 128].astype(F32) + ref[:, b : b + 128].astype(F32)
        last = ref[:, b - 128 : b].astype(F32) + ref[:, b + width - 128 :].astype(F32)
        left, right = strip_point(left, right, first, last, at, lane)
    for ref, v in ((ml_ref, left), (mr_ref, right)):
        hi = v.astype(BF16).astype(F32)
        ref[:, 128:] = (hi + roll(v - hi, 1)).astype(BF16)


def gelu_parts(pre):
    cdf = 0.5 * (1.0 + lax.erf(pre * 0.7071067811865476))
    return pre * cdf, cdf


def main_kernel(
    flags, *refs, inv_npix, count,
):
    hbm, refs = refs[:count], refs[count:]
    out_ref, x3, h3, d3, grad, s2, dpre2, wide, tr, sem, *refs = refs
    copies = [pltpu.make_async_copy(a, b, sem.at[i]) for i, (a, b) in enumerate(zip(hbm, refs))]
    for c in copies:
        c.start()
    ls_ref, rs_ref, ml_ref, mr_ref, k_ref, g_ref, x2_ref, top_ref, bot_ref, pt_ref, proj_ref, t_ref = refs
    for c in copies[:-3]:
        c.wait()
    chans = x2_ref.shape[0]
    width = top_ref.shape[1] // 5
    height = x2_ref.shape[1] // width
    has_up, has_dn = flags[0].astype(F32), flags[1].astype(F32)
    has_l, has_r = flags[2].astype(F32), flags[3].astype(F32)
    lane = lanes_of((chans, 128))
    kin, kout, kback = k_ref[0], k_ref[1], k_ref[2]
    gram = g_ref[...]

    def taps(v):
        return jnp.concatenate(
            [roll(v, -(a * PITCH + b)) for a in range(3) for b in range(3)], 0
        ).astype(BF16)

    col = lax.rem(lane, PITCH)
    rowi = lax.div(lane, PITCH)
    halo_l = ls_ref[:, :128].astype(F32)
    halo_r = rs_ref[:, :128].astype(F32)
    strip = jnp.concatenate(
        [
            jnp.where(col < 3, halo_l, roll(ml_ref[:, :128].astype(F32), 1)),
            jnp.where(col >= 2, halo_r, roll(mr_ref[:, :128].astype(F32), -1)),
        ],
        1,
    )
    lane2 = lanes_of((1, 128))
    col1 = lax.rem(lane2, PITCH)
    row1 = lax.div(lane2, PITCH)

    def row_mask(rim):
        inside = jnp.where(row1 < rim, has_up, 1.0)
        return jnp.where(row1 >= height + rim, has_dn, inside)

    hid, _ = gelu_parts(dot(kin, taps(strip)))
    mask = row_mask(2)
    mask = jnp.concatenate(
        [mask * jnp.where(col1 < 2, has_l, 1.0), mask * jnp.where(col1 >= 1, has_r, 1.0)], 1
    )
    hid = (hid * mask).astype(BF16).astype(F32)
    stud = (roll(strip, -(2 * PITCH + 2)) + dot(kout, taps(hid))).astype(BF16)
    halves = jnp.concatenate([ls_ref[:, 128:].astype(F32), rs_ref[:, 128:].astype(F32)], 1)
    pts = halves + roll(halves, -1)
    ds_strip = (dot(gram, jnp.concatenate([stud, stud], 0)) - pts) * inv_npix
    mask = row_mask(1)
    ds_strip = ds_strip * jnp.concatenate([mask * has_l, mask * has_r], 1)
    ds_strip = ds_strip.astype(BF16).astype(F32)

    def put(dst, r, seg, left, at_l, right, at_r):
        lo, hi = r * width, (r + 1) * width
        seg32 = seg.astype(F32)
        ahead = roll(seg32, 1)
        first = jnp.where(lane == 0, roll(left, -at_l), ahead[:, :128])
        dst[0:chans, lo : lo + 128] = first.astype(BF16)
        dst[0:chans, lo + 128 : hi] = ahead[:, 128:].astype(BF16)
        dst[chans : 2 * chans, lo:hi] = seg
        back = roll(seg32, -1)
        last = jnp.where(lane == 127, roll(right, 127 - at_r), back[:, width - 128 :])
        dst[2 * chans :, lo : hi - 128] = back[:, : width - 128].astype(BF16)
        dst[2 * chans :, hi - 128 : hi] = last.astype(BF16)

    def rows3(src, r):
        return jnp.concatenate(
            [src[:, (r + a) * width : (r + a + 1) * width] for a in range(3)], 0
        )

    for r in range(height + 6):
        if r < 3:
            seg = top_ref[:, r * width : (r + 1) * width]
        elif r < height + 3:
            seg = x2_ref[:, (r - 3) * width : (r - 2) * width]
        else:
            seg = bot_ref[:, (r - height - 3) * width : (r - height - 2) * width]
        put(x3, r, seg, halo_l, r * PITCH + 2, halo_r, r * PITCH + 2)

    for r in range(height + 4):
        pre = dot(kin, rows3(x3, r))
        hid_r, cdf = gelu_parts(pre)
        if r < 2:
            hid_r = hid_r * has_up
        elif r >= height + 2:
            hid_r = hid_r * has_dn
        else:
            dens = jnp.exp(-0.5 * pre * pre) * 0.3989422804014327
            grad[:, (r - 2) * width : (r - 1) * width] = cdf + pre * dens
        at = r * PITCH + 1
        put(h3, r, hid_r.astype(BF16), hid[:, :128], at, hid[:, 128:], at)

    for r in range(height + 2):
        seg = x3[chans : 2 * chans, (r + 2) * width : (r + 3) * width]
        stud = (seg.astype(F32) + dot(kout, rows3(h3, r))).astype(BF16)
        s2[:chans, r * width : (r + 1) * width] = stud
        s2[chans:, r * width : (r + 1) * width] = stud

    copies[-3].wait()
    for r in range(height + 2):
        if r == 0:
            pt = top_ref[:, 3 * width : 4 * width].astype(F32) + top_ref[:, 4 * width :].astype(F32)
        elif r == height + 1:
            pt = bot_ref[:, 3 * width : 4 * width].astype(F32) + bot_ref[:, 4 * width :].astype(F32)
        else:
            pt = pt_ref[:, (r - 1) * width : r * width]
        ds = (dot(gram, s2[:, r * width : (r + 1) * width]) - pt) * inv_npix
        if r == 0:
            ds = ds * has_up
        elif r == height + 1:
            ds = ds * has_dn
        at = r * PITCH
        put(d3, r, ds.astype(BF16), ds_strip[:, :128], at, ds_strip[:, 128:], at)

    for r in range(height):
        span = slice(r * width, (r + 1) * width)
        dpre2[:, span] = (dot(kback, rows3(d3, r)) * grad[:, span]).astype(BF16)

    pixels = height * width
    per = 3 * chans
    quarter = 9 * chans // 4
    piece = chans // 3
    for n, (src, lag, grads) in enumerate(
        ((x3, 2, dpre2[...]), (h3, 1, d3[chans : 2 * chans, width : width + pixels]))
    ):
        for a in range(3):
            base = (a + lag) * width
            wide[a * per : (a + 1) * per, :chans] = dot_nt(src[:, base : base + pixels], grads)
        for k in range(3):
            at = (3 * n + k) * quarter
            rows = wide[k * quarter : (k + 1) * quarter, :]
            extra = roll(wide[3 * quarter : 4 * quarter, :], chans - k * piece)
            lane_q = lanes_of((quarter, 128))
            out_ref[at : at + quarter, :] = jnp.where(lane_q < chans, rows, extra)

    copies[-2].wait()
    copies[-1].wait()
    stud = s2[:chans, width : width + pixels]
    hi, lo = split(dot_nt(stud, stud))
    proj = proj_ref[...]
    gp = dot(jnp.concatenate([hi, lo], 1), jnp.concatenate([proj, proj], 0))
    parts, step = tr.shape[0], tr.shape[1]
    start = 6 * quarter
    for k in range(t_ref.shape[0] // step):
        rows = jnp.swapaxes(t_ref[k * step : (k + 1) * step], 0, 1)
        for h in range(height):
            tr[k % parts, :, h * width : (h + 1) * width] = rows[h]
        cross = dot_nt(tr[k % parts], stud)
        for j in range(k * step // 128, (k + 1) * step // 128):
            lo = j * 128 - k * step
            part = gp[:, j * 128 : (j + 1) * 128] - cross[lo : lo + 128].T
            out_ref[start + j * chans : start + (j + 1) * chans, :] = part * inv_npix
    end = start + t_ref.shape[0] // 128 * chans
    out_ref[end:, :] = jnp.zeros((out_ref.shape[0] - end, 128), F32)


def unpack_kernel(v_ref, gin_ref, gout_ref, gproj_ref):
    chans = gproj_ref.shape[0]
    quarter = 9 * chans // 4
    piece = chans // 3
    for n, ref in enumerate((gin_ref, gout_ref)):
        for k in range(3):
            at = (3 * n + k) * quarter
            ref[k * quarter : (k + 1) * quarter, :] = v_ref[at : at + quarter, :chans]
            ref[3 * quarter :, k * piece : (k + 1) * piece] = v_ref[at : at + quarter, chans:]
    start = 6 * quarter
    for j in range(gproj_ref.shape[1] // 128):
        at = start + j * chans
        gproj_ref[:, j * 128 : (j + 1) * 128] = v_ref[at : at + chans, :]


VMEM = pl.BlockSpec(memory_space=pltpu.VMEM)
ANY = pl.BlockSpec(memory_space=pl.ANY)


def grant(mib):
    return pltpu.CompilerParams(vmem_limit_bytes=mib << 20)


def swap(v, axis, bit):
    return lax.ppermute(v, axis, [(i, i ^ bit) for i in range(lax.axis_size(axis))])


def bits_of(axis):
    return [1 << k for k in range(lax.axis_size(axis).bit_length() - 1)]


def sum_all(v):
    col, row = bits_of("col"), bits_of("row")
    halved = [("col", col[0], 0), ("col", col[1], 0), ("row", row[0], 0)]
    rest = [("col", b) for b in col[2:]] + [("row", b) for b in row[1:]]
    for axis, bit, dim in halved:
        mine = (lax.axis_index(axis) & bit) // bit
        half = v.shape[dim] // 2
        give = lax.dynamic_slice_in_dim(v, (1 - mine) * half, half, dim)
        keep = lax.dynamic_slice_in_dim(v, mine * half, half, dim)
        v = keep + swap(give, axis, bit)
    for axis, bit in rest:
        v = v + swap(v, axis, bit)
    for axis, bit, dim in halved[::-1]:
        got = swap(v, axis, bit)
        upper = (lax.axis_index(axis) & bit) != 0
        v = jnp.concatenate([jnp.where(upper, got, v), jnp.where(upper, v, got)], dim)
    return v


def shift(v, axis, by):
    n = lax.axis_size(axis)
    return lax.ppermute(v, axis, [(i, i + by) for i in range(n) if 0 <= i + by < n])


def shards(features, teacher, conv_in, conv_out, projector):
    chans, height, width = features.shape
    ends = teacher.shape[0]
    pixels = height * width
    parts = 6
    x2, pt, gram, up, dn, own, kernels = pl.pallas_call(
        teach_kernel,
        in_specs=[VMEM] * 4 + [ANY],
        out_specs=[VMEM] * 7,
        out_shape=[
            jax.ShapeDtypeStruct((chans, pixels), BF16),
            jax.ShapeDtypeStruct((chans, pixels), F32),
            jax.ShapeDtypeStruct((chans, 2 * chans), BF16),
            jax.ShapeDtypeStruct((chans, 5 * width), BF16),
            jax.ShapeDtypeStruct((chans, 5 * width), BF16),
            jax.ShapeDtypeStruct((4, chans, 128), F32),
            jax.ShapeDtypeStruct((3, chans, 9 * chans), BF16),
        ],
        scratch_shapes=[
            pltpu.VMEM((ends, height, width), BF16),
            pltpu.VMEM((2, ends // parts, pixels), BF16),
            pltpu.SemaphoreType.DMA((parts,)),
        ],
        compiler_params=grant(60),
        name="teach",
    )(features, projector, conv_in, conv_out, teacher)
    bot = shift(up, "row", -1)
    top = shift(dn, "row", 1)
    ml, mr = pl.pallas_call(
        functools.partial(strip_kernel, height=height),
        in_specs=[VMEM] * 3,
        out_specs=[VMEM] * 2,
        out_shape=[jax.ShapeDtypeStruct((chans, 256), BF16)] * 2,
        compiler_params=grant(8),
        name="strips",
    )(own, top, bot)
    rs = shift(ml, "col", -1)
    ls = shift(mr, "col", 1)
    row, col = lax.axis_index("row"), lax.axis_index("col")
    flags = jnp.stack(
        [row > 0, row < lax.axis_size("row") - 1, col > 0, col < lax.axis_size("col") - 1]
    ).astype(jnp.int32)
    npix = pixels * lax.axis_size("row") * lax.axis_size("col")
    total = 2 * 9 * chans * chans // 128 + ends // 128 * chans
    total = -(-total // 64) * 64
    arrays = (ls, rs, ml, mr, kernels, gram, x2, top, bot, pt, projector, teacher)
    v = pl.pallas_call(
        functools.partial(main_kernel, inv_npix=1.0 / npix, count=len(arrays)),
        in_specs=[pl.BlockSpec(memory_space=pltpu.SMEM)] + [ANY] * len(arrays),
        out_specs=VMEM,
        out_shape=jax.ShapeDtypeStruct((total, 128), F32),
        scratch_shapes=[
            pltpu.VMEM((3 * chans, (height + 6) * width), BF16),
            pltpu.VMEM((3 * chans, (height + 4) * width), BF16),
            pltpu.VMEM((3 * chans, (height + 2) * width), BF16),
            pltpu.VMEM((chans, pixels), F32),
            pltpu.VMEM((2 * chans, (height + 2) * width), BF16),
            pltpu.VMEM((chans, pixels), BF16),
            pltpu.VMEM((9 * chans, 128), F32),
            pltpu.VMEM((2, ends // parts, pixels), BF16),
            pltpu.SemaphoreType.DMA((len(arrays),)),
        ]
        + [pltpu.VMEM(a.shape, a.dtype) for a in arrays],
        compiler_params=grant(60),
        name="block",
    )(flags, *arrays)
    v = sum_all(v)
    gin, gout, gproj = pl.pallas_call(
        unpack_kernel,
        in_specs=[VMEM],
        out_specs=[VMEM] * 3,
        out_shape=[
            jax.ShapeDtypeStruct((9 * chans, chans), F32),
            jax.ShapeDtypeStruct((9 * chans, chans), F32),
            jax.ShapeDtypeStruct((chans, ends), F32),
        ],
        compiler_params=grant(12),
        name="unpack",
    )(v)
    return gin.reshape(9, chans, chans), gout.reshape(9, chans, chans), gproj


def solution(mesh):
    in_specs = (P(None, "row", "col"), P(None, "row", "col"), P(), P(), P())
    out_specs = (P(), P(), P())
    return jax.shard_map(shards, mesh=mesh, in_specs=in_specs, out_specs=out_specs, check_vma=False)
```

```python
import functools

import jax
import jax.numpy as jnp
from jax import lax
from jax.experimental import pallas as pl
from jax.experimental.pallas import tpu as pltpu
from jax.sharding import PartitionSpec as P

F32 = jnp.float32
BF16 = jnp.bfloat16
PITCH = 3
RIGHT = 64


def dot(a, b):
    return jnp.dot(a, b, preferred_element_type=F32)


def dot_nt(a, b):
    return lax.dot_general(a, b, (((1,), (1,)), ((), ())), preferred_element_type=F32)


def split(v):
    hi = v.astype(BF16)
    return hi, (v - hi.astype(F32)).astype(BF16)


def lanes_of(shape):
    return lax.broadcasted_iota(jnp.int32, shape, 1)


def roll(v, by):
    by = by % v.shape[1]
    return v if by == 0 else pltpu.roll(v, by, 1)


def weight_kernel(cin_ref, cout_ref, p_ref, k_ref, pt_ref):
    k_ref[0] = jnp.concatenate([cin_ref[t].T for t in range(9)], 1)
    k_ref[1] = jnp.concatenate([cout_ref[t].T for t in range(9)], 1)
    k_ref[2] = jnp.concatenate([cout_ref[8 - t] for t in range(9)], 1)
    pt_ref[...] = p_ref[...].T


def feature_kernel(x_ref, x2_ref, up_ref, dn_ref):
    height, width = x_ref.shape[1:]
    rows = jnp.swapaxes(x_ref[...], 0, 1)
    for h in range(height):
        x2_ref[:, h * width : (h + 1) * width] = rows[h]
    for h in range(2):
        up_ref[:, h * width : (h + 1) * width] = rows[h]
        dn_ref[:, h * width : (h + 1) * width] = rows[height - 2 + h]


def strip_kernel(x2_ref, top_ref, bot_ref, ml_ref, mr_ref, own_ref):
    chans = x2_ref.shape[0]
    width = top_ref.shape[1] // 2
    height = x2_ref.shape[1] // width
    lane = lanes_of((chans, 128))
    left = right = own = jnp.zeros((chans, 128), F32)
    for r in range(height + 4):
        if r < 2:
            ref, base = top_ref, r * width
        elif r < height + 2:
            ref, base = x2_ref, (r - 2) * width
        else:
            ref, base = bot_ref, (r - height - 2) * width
        first = ref[:, base : base + 128].astype(F32)
        last = ref[:, base + width - 128 : base + width].astype(F32)
        at = r * PITCH
        left = jnp.where((lane >= at + 1) & (lane < at + 3), roll(first, at + 1), left)
        right = jnp.where((lane >= at) & (lane < at + 2), roll(last, at - 126), right)
        own = jnp.where(lane == at + 2, roll(first, at + 2), own)
        own = jnp.where(lane == at + RIGHT, roll(last, at + RIGHT - 127), own)
    ml_ref[...] = left.astype(BF16)
    mr_ref[...] = right.astype(BF16)
    own_ref[...] = own.astype(BF16)


def gelu_and_slope(pre):
    cdf = 0.5 * (1.0 + lax.erf(pre * 0.7071067811865476))
    dens = jnp.exp(-0.5 * pre * pre) * 0.3989422804014327
    return pre * cdf, cdf + pre * dens


def main_kernel(flags, *refs, inv_npix, count):
    hbm, refs = refs[:count], refs[count:]
    out_ref, x3, h3, d3, grad, s2, dpre2, wide, gp, tr, sem, *refs = refs
    parts = sem.shape[0] - count + 1
    copies = [
        pltpu.make_async_copy(a, b, sem.at[i]) for i, (a, b) in enumerate(zip(hbm[:-1], refs))
    ]
    for c in copies:
        c.start()
    k_ref, x2_ref, own_ref, ls_ref, rs_ref, top_ref, bot_ref, pt_ref, proj_ref, t_ref = refs
    ends = t_ref.shape[0]
    step = ends // parts
    pieces = [
        pltpu.make_async_copy(
            hbm[-1].at[pl.ds(k * step, step)],
            t_ref.at[pl.ds(k * step, step)],
            sem.at[count - 1 + k],
        )
        for k in range(parts)
    ]
    for c in pieces:
        c.start()
    for c in copies[:-2]:
        c.wait()
    chans = x2_ref.shape[0]
    width = top_ref.shape[1] // 2
    height = x2_ref.shape[1] // width
    pixels = height * width
    has_up, has_dn = flags[0].astype(F32), flags[1].astype(F32)
    has_l, has_r = flags[2].astype(F32), flags[3].astype(F32)
    lane = lanes_of((chans, 128))
    kin, kout, kback = k_ref[0], k_ref[1], k_ref[2]

    def taps(v):
        return jnp.concatenate(
            [roll(v, -(a * PITCH + b)) for a in range(3) for b in range(3)], 0
        ).astype(BF16)

    part = lax.rem(lane, RIGHT)
    col = lax.rem(part, PITCH)
    halo_l, halo_r = ls_ref[...].astype(F32), roll(rs_ref[...].astype(F32), RIGHT)
    strip = jnp.where(lane < RIGHT, jnp.where(col < 2, halo_l, 0.0), jnp.where(col > 0, halo_r, 0.0))
    strip = jnp.where(part < (height + 4) * PITCH, strip, 0.0) + own_ref[...].astype(F32)
    strip_taps = taps(strip)
    lane1 = lanes_of((1, 128))
    part1 = lax.rem(lane1, RIGHT)
    mask = jnp.where(part1 == 0, has_up, jnp.where(part1 == (height + 1) * PITCH, has_dn, 1.0))
    mask = jnp.where(lane1 < RIGHT, mask * has_l, mask * has_r)
    mask = jnp.where((lax.rem(part1, PITCH) == 0) & (part1 < (height + 2) * PITCH), mask, 0.0)
    hid_s, grad_s = gelu_and_slope(dot(kin, strip_taps))
    hid_s = (hid_s * mask).astype(BF16).astype(F32)
    grad_s = grad_s * mask

    def put(dst, r, seg, rim, at):
        lo, hi = r * width, (r + 1) * width
        seg32 = seg.astype(F32)
        ahead = roll(seg32, 1)
        first = roll(rim, -at) if rim is not None else 0.0
        first = jnp.where(lane == 0, first, ahead[:, :128])
        dst[0:chans, lo : lo + 128] = first.astype(BF16)
        dst[0:chans, lo + 128 : hi] = ahead[:, 128:].astype(BF16)
        dst[chans : 2 * chans, lo:hi] = seg
        back = roll(seg32, -1)
        last = roll(rim, 127 - RIGHT - at) if rim is not None else 0.0
        last = jnp.where(lane == 127, last, back[:, width - 128 :])
        dst[2 * chans :, lo : hi - 128] = back[:, : width - 128].astype(BF16)
        dst[2 * chans :, hi - 128 : hi] = last.astype(BF16)

    def rows3(src, r):
        return jnp.concatenate(
            [src[:, (r + a) * width : (r + a + 1) * width] for a in range(3)], 0
        )

    for r in range(height + 4):
        if r < 2:
            seg = top_ref[:, r * width : (r + 1) * width]
        elif r < height + 2:
            seg = x2_ref[:, (r - 2) * width : (r - 1) * width]
        else:
            seg = bot_ref[:, (r - height - 2) * width : (r - height - 1) * width]
        put(x3, r, seg, strip, r * PITCH + 1)

    for r in range(height + 2):
        hid, slope = gelu_and_slope(dot(kin, rows3(x3, r)))
        if r == 0:
            hid, slope = hid * has_up, slope * has_up
        elif r == height + 1:
            hid, slope = hid * has_dn, slope * has_dn
        grad[:, r * width : (r + 1) * width] = slope
        put(h3, r, hid.astype(BF16), hid_s, r * PITCH)

    for r in range(height):
        span = slice(r * width, (r + 1) * width)
        seg = x2_ref[:, span].astype(F32)
        s2[:, span] = (seg + dot(kout, rows3(h3, r))).astype(BF16)

    for k in range(parts):
        pieces[k].wait()
        rows = jnp.swapaxes(t_ref[k * step : (k + 1) * step], 0, 1)
        for h in range(height):
            tr[k * step : (k + 1) * step, h * width : (h + 1) * width] = rows[h]

    for c in copies[-2:]:
        c.wait()
    proj_t, proj = pt_ref[...], proj_ref[...]
    rim = jnp.zeros((3 * chans, 2 * width), BF16)
    d3[:, : 2 * width] = rim
    d3[:, (height + 2) * width :] = rim
    ds_s = jnp.zeros((chans, 128), F32)
    for r in range(height):
        span = slice(r * width, (r + 1) * width)
        stud = s2[:, span]
        pred = dot(proj_t, stud)
        dpred = ((pred - tr[:, span].astype(F32)) * inv_npix).astype(BF16)
        cross = dot_nt(dpred, stud)
        if r == 0:
            gp[...] = cross
        else:
            gp[...] += cross
        ds = dot(proj, dpred).astype(BF16)
        put(d3, r + 2, ds, None, 0)
        at = (r + 2) * PITCH
        ds32 = ds.astype(F32)
        ds_s = jnp.where(lane == at + 2, roll(ds32[:, :128], at + 2), ds_s)
        ds_s = jnp.where(lane == at + RIGHT, roll(ds32[:, width - 128 :], at + RIGHT - 127), ds_s)

    for r in range(height + 2):
        span = slice(r * width, (r + 1) * width)
        dpre2[:, span] = (dot(kback, rows3(d3, r)) * grad[:, span]).astype(BF16)
    dpre_s = (dot(kback, taps(ds_s)) * grad_s).astype(BF16)

    per = 3 * chans
    quarter = 9 * chans // 4
    piece = chans // 3
    lane_q = lanes_of((quarter, 128))
    for n in range(2):
        for a in range(3):
            base = a * width
            if n == 0:
                g = dot_nt(x3[:, base : base + pixels + 2 * width], dpre2[...])
                g += dot_nt(strip_taps[a * per : (a + 1) * per], dpre_s)
            else:
                grads = d3[chans : 2 * chans, 2 * width : 2 * width + pixels]
                g = dot_nt(h3[:, base : base + pixels], grads)
            wide[a * per : (a + 1) * per, :chans] = g
        for k in range(3):
            at = (3 * n + k) * quarter
            rows = wide[k * quarter : (k + 1) * quarter, :]
            extra = roll(wide[3 * quarter : 4 * quarter, :], chans - k * piece)
            out_ref[at : at + quarter, :] = jnp.where(lane_q < chans, rows, extra)

    start = 6 * quarter
    for j in range(ends // 128):
        at = start + j * chans
        out_ref[at : at + chans, :] = gp[j * 128 : (j + 1) * 128, :].T
    end = start + ends // 128 * chans
    out_ref[end:, :] = jnp.zeros((out_ref.shape[0] - end, 128), F32)


def unpack_kernel(v_ref, gin_ref, gout_ref, gproj_ref):
    chans = gproj_ref.shape[0]
    quarter = 9 * chans // 4
    piece = chans // 3
    for n, ref in enumerate((gin_ref, gout_ref)):
        for k in range(3):
            at = (3 * n + k) * quarter
            ref[k * quarter : (k + 1) * quarter, :] = v_ref[at : at + quarter, :chans]
            ref[3 * quarter :, k * piece : (k + 1) * piece] = v_ref[at : at + quarter, chans:]
    start = 6 * quarter
    for j in range(gproj_ref.shape[1] // 128):
        at = start + j * chans
        gproj_ref[:, j * 128 : (j + 1) * 128] = v_ref[at : at + chans, :]


VMEM = pl.BlockSpec(memory_space=pltpu.VMEM)
ANY = pl.BlockSpec(memory_space=pl.ANY)


def grant(mib):
    return pltpu.CompilerParams(vmem_limit_bytes=mib << 20)


def swap(v, bits):
    n = lax.axis_size("row") * lax.axis_size("col")
    return lax.ppermute(v, ("row", "col"), [(i, i ^ bits[i & 1]) for i in range(n)])


def sum_all(v):
    me = lax.axis_index("row") * lax.axis_size("col") + lax.axis_index("col")
    n = lax.axis_size("row") * lax.axis_size("col")
    bits = [1 << k for k in range(1, n.bit_length() - 1)]
    steps = [(1, 1)]
    for k in range(len(bits)):
        other = k ^ 1 if k ^ 1 < len(bits) else k
        steps.append((bits[k], bits[other]))
    halved, rest = steps[:3], steps[3:]

    def upper(pair):
        return (me & jnp.where(me % 2 == 0, pair[0], pair[1])) != 0

    for pair in halved:
        mine = upper(pair).astype(jnp.int32)
        half = v.shape[0] // 2
        give = lax.dynamic_slice_in_dim(v, (1 - mine) * half, half, 0)
        keep = lax.dynamic_slice_in_dim(v, mine * half, half, 0)
        v = keep + swap(give, pair)
    for pair in rest:
        v = v + swap(v, pair)
    for pair in halved[::-1]:
        got = swap(v, pair)
        top = upper(pair)
        v = jnp.concatenate([jnp.where(top, got, v), jnp.where(top, v, got)], 0)
    return v


def shift(v, axis, by):
    n = lax.axis_size(axis)
    return lax.ppermute(v, axis, [(i, i + by) for i in range(n) if 0 <= i + by < n])


def shards(features, teacher, conv_in, conv_out, projector):
    chans, height, width = features.shape
    ends = teacher.shape[0]
    pixels = height * width
    parts = 6
    x2, up, dn = pl.pallas_call(
        feature_kernel,
        in_specs=[VMEM],
        out_specs=[VMEM] * 3,
        out_shape=[
            jax.ShapeDtypeStruct((chans, pixels), BF16),
            jax.ShapeDtypeStruct((chans, 2 * width), BF16),
            jax.ShapeDtypeStruct((chans, 2 * width), BF16),
        ],
        compiler_params=grant(8),
        name="features",
    )(features)
    bot = shift(up, "row", -1)
    top = shift(dn, "row", 1)
    kernels, proj_t = pl.pallas_call(
        weight_kernel,
        in_specs=[VMEM] * 3,
        out_specs=[VMEM] * 2,
        out_shape=[
            jax.ShapeDtypeStruct((3, chans, 9 * chans), BF16),
            jax.ShapeDtypeStruct((ends, chans), BF16),
        ],
        compiler_params=grant(8),
        name="weights",
    )(conv_in, conv_out, projector)
    ml, mr, own = pl.pallas_call(
        strip_kernel,
        in_specs=[VMEM] * 3,
        out_specs=[VMEM] * 3,
        out_shape=[jax.ShapeDtypeStruct((chans, 128), BF16)] * 3,
        compiler_params=grant(8),
        name="strips",
    )(x2, top, bot)
    rs = shift(ml, "col", -1)
    ls = shift(mr, "col", 1)
    row, col = lax.axis_index("row"), lax.axis_index("col")
    flags = jnp.stack(
        [row > 0, row < lax.axis_size("row") - 1, col > 0, col < lax.axis_size("col") - 1]
    ).astype(jnp.int32)
    npix = pixels * lax.axis_size("row") * lax.axis_size("col")
    total = 2 * 9 * chans * chans // 128 + ends // 128 * chans
    total = -(-total // 64) * 64
    arrays = (kernels, x2, own, ls, rs, top, bot, proj_t, projector, teacher)
    v = pl.pallas_call(
        functools.partial(main_kernel, inv_npix=1.0 / npix, count=len(arrays)),
        in_specs=[pl.BlockSpec(memory_space=pltpu.SMEM)] + [ANY] * len(arrays),
        out_specs=VMEM,
        out_shape=jax.ShapeDtypeStruct((total, 128), F32),
        scratch_shapes=[
            pltpu.VMEM((3 * chans, (height + 4) * width), BF16),
            pltpu.VMEM((3 * chans, (height + 2) * width), BF16),
            pltpu.VMEM((3 * chans, (height + 4) * width), BF16),
            pltpu.VMEM((chans, (height + 2) * width), F32),
            pltpu.VMEM((chans, pixels), BF16),
            pltpu.VMEM((chans, (height + 2) * width), BF16),
            pltpu.VMEM((9 * chans, 128), F32),
            pltpu.VMEM((ends, chans), F32),
            pltpu.VMEM((ends, pixels), BF16),
            pltpu.SemaphoreType.DMA((len(arrays) - 1 + parts,)),
        ]
        + [pltpu.VMEM(a.shape, a.dtype) for a in arrays],
        compiler_params=grant(60),
        name="block",
    )(flags, *arrays)
    v = sum_all(v)
    gin, gout, gproj = pl.pallas_call(
        unpack_kernel,
        in_specs=[VMEM],
        out_specs=[VMEM] * 3,
        out_shape=[
            jax.ShapeDtypeStruct((9 * chans, chans), F32),
            jax.ShapeDtypeStruct((9 * chans, chans), F32),
            jax.ShapeDtypeStruct((chans, ends), F32),
        ],
        compiler_params=grant(12),
        name="unpack",
    )(v)
    return gin.reshape(9, chans, chans), gout.reshape(9, chans, chans), gproj


def solution(mesh):
    in_specs = (P(None, "row", "col"), P(None, "row", "col"), P(), P(), P())
    out_specs = (P(), P(), P())
    return jax.shard_map(shards, mesh=mesh, in_specs=in_specs, out_specs=out_specs, check_vma=False)
```

```python
import functools

import jax
import jax.numpy as jnp
from jax import lax
from jax.experimental import pallas as pl
from jax.experimental.pallas import tpu as pltpu
from jax.sharding import PartitionSpec as P

F32 = jnp.float32
BF16 = jnp.bfloat16
PITCH = 3
RIGHT = 64


def dot(a, b):
    return jnp.dot(a, b, preferred_element_type=F32)


def dot_nt(a, b):
    return lax.dot_general(a, b, (((1,), (1,)), ((), ())), preferred_element_type=F32)


def split(v):
    hi = v.astype(BF16)
    return hi, (v - hi.astype(F32)).astype(BF16)


def lanes_of(shape):
    return lax.broadcasted_iota(jnp.int32, shape, 1)


def roll(v, by):
    by = by % v.shape[1]
    return v if by == 0 else pltpu.roll(v, by, 1)


def weight_kernel(cin_ref, cout_ref, p_ref, k_ref, pt_ref):
    k_ref[0] = jnp.concatenate([cin_ref[t].T for t in range(9)], 1)
    k_ref[1] = jnp.concatenate([cout_ref[t].T for t in range(9)], 1)
    k_ref[2] = jnp.concatenate([cout_ref[8 - t] for t in range(9)], 1)
    pt_ref[...] = p_ref[...].T


def feature_kernel(x_ref, x2_ref, up_ref, dn_ref):
    height, width = x_ref.shape[1:]
    rows = jnp.swapaxes(x_ref[...], 0, 1)
    for h in range(height):
        x2_ref[:, h * width : (h + 1) * width] = rows[h]
    for h in range(2):
        up_ref[:, h * width : (h + 1) * width] = rows[h]
        dn_ref[:, h * width : (h + 1) * width] = rows[height - 2 + h]


def strip_kernel(x2_ref, top_ref, bot_ref, ml_ref, mr_ref, own_ref):
    chans = x2_ref.shape[0]
    width = top_ref.shape[1] // 2
    height = x2_ref.shape[1] // width
    lane = lanes_of((chans, 128))
    left = right = own = jnp.zeros((chans, 128), F32)
    for r in range(height + 4):
        if r < 2:
            ref, base = top_ref, r * width
        elif r < height + 2:
            ref, base = x2_ref, (r - 2) * width
        else:
            ref, base = bot_ref, (r - height - 2) * width
        first = ref[:, base : base + 128].astype(F32)
        last = ref[:, base + width - 128 : base + width].astype(F32)
        at = r * PITCH
        left = jnp.where((lane >= at + 1) & (lane < at + 3), roll(first, at + 1), left)
        right = jnp.where((lane >= at) & (lane < at + 2), roll(last, at - 126), right)
        own = jnp.where(lane == at + 2, roll(first, at + 2), own)
        own = jnp.where(lane == at + RIGHT, roll(last, at + RIGHT - 127), own)
    ml_ref[...] = left.astype(BF16)
    mr_ref[...] = right.astype(BF16)
    own_ref[...] = own.astype(BF16)


def gelu_and_slope(pre):
    cdf = 0.5 * (1.0 + lax.erf(pre * 0.7071067811865476))
    dens = jnp.exp(-0.5 * pre * pre) * 0.3989422804014327
    return pre * cdf, cdf + pre * dens


def main_kernel(flags, *refs, inv_npix, count):
    hbm, refs = refs[:count], refs[count:]
    out_ref, x3, h3, d3, grad, s2, dpre2, ds2, wide, gp, tr, sem, *refs = refs
    parts = sem.shape[0] - count + 1
    copies = [
        pltpu.make_async_copy(a, b, sem.at[i]) for i, (a, b) in enumerate(zip(hbm[:-1], refs))
    ]
    for c in copies:
        c.start()
    k_ref, x2_ref, own_ref, ls_ref, rs_ref, top_ref, bot_ref, pt_ref, proj_ref, t_ref = refs
    ends = t_ref.shape[0]
    step = ends // parts
    pieces = [
        pltpu.make_async_copy(
            hbm[-1].at[pl.ds(k * step, step)],
            t_ref.at[pl.ds(k * step, step)],
            sem.at[count - 1 + k],
        )
        for k in range(parts)
    ]
    for c in pieces:
        c.start()
    for c in copies[:-2]:
        c.wait()
    chans = x2_ref.shape[0]
    width = top_ref.shape[1] // 2
    height = x2_ref.shape[1] // width
    pixels = height * width
    has_up, has_dn = flags[0].astype(F32), flags[1].astype(F32)
    has_l, has_r = flags[2].astype(F32), flags[3].astype(F32)
    lane = lanes_of((chans, 128))
    kin, kout, kback = k_ref[0], k_ref[1], k_ref[2]

    def taps(v):
        return jnp.concatenate(
            [roll(v, -(a * PITCH + b)) for a in range(3) for b in range(3)], 0
        ).astype(BF16)

    part = lax.rem(lane, RIGHT)
    col = lax.rem(part, PITCH)
    halo_l, halo_r = ls_ref[...].astype(F32), roll(rs_ref[...].astype(F32), RIGHT)
    strip = jnp.where(lane < RIGHT, jnp.where(col < 2, halo_l, 0.0), jnp.where(col > 0, halo_r, 0.0))
    strip = jnp.where(part < (height + 4) * PITCH, strip, 0.0) + own_ref[...].astype(F32)
    strip_taps = taps(strip)
    lane1 = lanes_of((1, 128))
    part1 = lax.rem(lane1, RIGHT)
    mask = jnp.where(part1 == 0, has_up, jnp.where(part1 == (height + 1) * PITCH, has_dn, 1.0))
    mask = jnp.where(lane1 < RIGHT, mask * has_l, mask * has_r)
    mask = jnp.where((lax.rem(part1, PITCH) == 0) & (part1 < (height + 2) * PITCH), mask, 0.0)
    hid_s, grad_s = gelu_and_slope(dot(kin, strip_taps))
    hid_s = (hid_s * mask).astype(BF16).astype(F32)
    grad_s = grad_s * mask

    def put(dst, r, seg, rim, at):
        lo, hi = r * width, (r + 1) * width
        seg32 = seg.astype(F32)
        ahead = roll(seg32, 1)
        first = roll(rim, -at) if rim is not None else 0.0
        first = jnp.where(lane == 0, first, ahead[:, :128])
        dst[0:chans, lo : lo + 128] = first.astype(BF16)
        dst[0:chans, lo + 128 : hi] = ahead[:, 128:].astype(BF16)
        dst[chans : 2 * chans, lo:hi] = seg
        back = roll(seg32, -1)
        last = roll(rim, 127 - RIGHT - at) if rim is not None else 0.0
        last = jnp.where(lane == 127, last, back[:, width - 128 :])
        dst[2 * chans :, lo : hi - 128] = back[:, : width - 128].astype(BF16)
        dst[2 * chans :, hi - 128 : hi] = last.astype(BF16)

    def rows3(src, r):
        return jnp.concatenate(
            [src[:, (r + a) * width : (r + a + 1) * width] for a in range(3)], 0
        )

    for r in range(height + 4):
        if r < 2:
            seg = top_ref[:, r * width : (r + 1) * width]
        elif r < height + 2:
            seg = x2_ref[:, (r - 2) * width : (r - 1) * width]
        else:
            seg = bot_ref[:, (r - height - 2) * width : (r - height - 1) * width]
        put(x3, r, seg, strip, r * PITCH + 1)

    def teach(k):
        pieces[k].wait()
        rows = jnp.swapaxes(t_ref[k * step : (k + 1) * step], 0, 1)
        for h in range(height):
            tr[k * step : (k + 1) * step, h * width : (h + 1) * width] = rows[h]

    for r in range(height + 2):
        hid, slope = gelu_and_slope(dot(kin, rows3(x3, r)))
        if r == 0:
            hid, slope = hid * has_up, slope * has_up
        elif r == height + 1:
            hid, slope = hid * has_dn, slope * has_dn
        grad[:, r * width : (r + 1) * width] = slope
        put(h3, r, hid.astype(BF16), hid_s, r * PITCH)

    for r in range(height):
        span = slice(r * width, (r + 1) * width)
        seg = x2_ref[:, span].astype(F32)
        s2[:, span] = (seg + dot(kout, rows3(h3, r))).astype(BF16)
        if r % 2 == 1 and r < 12:
            teach(r // 2)

    for c in copies[-2:]:
        c.wait()
    proj_t, proj = pt_ref[...], proj_ref[...]
    rim = jnp.zeros((3 * chans, 2 * width), BF16)
    d3[:, : 2 * width] = rim
    d3[:, (height + 2) * width :] = rim
    ds_s = jnp.zeros((chans, 128), F32)
    group = width
    count = pixels // group

    def predict(k):
        return dot(proj_t, s2[:, k * group : (k + 1) * group])

    pred = predict(0)
    for k in range(count):
        span = slice(k * group, (k + 1) * group)
        following = predict(min(k + 1, count - 1))
        dpred = (pred - tr[:, span].astype(F32)).astype(BF16)
        cross = dot_nt(dpred, s2[:, span])
        if k == 0:
            gp[...] = cross
        else:
            gp[...] += cross
        ds_k = (dot(proj, dpred) * inv_npix).astype(BF16)
        pred = following
        for r in range(k * group // width, (k + 1) * group // width):
            at = r * width - k * group
            ds = ds_k[:, at : at + width]
            put(d3, r + 2, ds, None, 0)
            ds2[:chans, r * width : (r + 1) * width] = ds
            ds2[chans:, (r + 1) * width : (r + 2) * width] = ds
            at = (r + 2) * PITCH
            ds32 = ds.astype(F32)
            ds_s = jnp.where(lane == at + 2, roll(ds32[:, :128], at + 2), ds_s)
            ds_s = jnp.where(lane == at + RIGHT, roll(ds32[:, width - 128 :], at + RIGHT - 127), ds_s)

    blank = jnp.zeros((chans, width), BF16)
    for pair, last in ((dpre2, height + 2), (ds2, height)):
        pair[:chans, last * width :] = blank
        pair[chans:, :width] = blank

    for r in range(height + 2):
        span = slice(r * width, (r + 1) * width)
        dpre = (dot(kback, rows3(d3, r)) * grad[:, span]).astype(BF16)
        dpre2[:chans, span] = dpre
        dpre2[chans:, (r + 1) * width : (r + 2) * width] = dpre
    dpre_s = (dot(kback, taps(ds_s)) * grad_s).astype(BF16)

    per = 3 * chans
    quarter = 9 * chans // 4
    piece = chans // 3
    lane_q = lanes_of((quarter, 128))
    for n, (src, pair) in enumerate(((x3, dpre2), (h3, ds2))):
        size = pair.shape[1]
        both = dot_nt(src[:, :size], pair[...])
        third = dot_nt(src[:, 2 * width : width + size], pair[:chans, : size - width])
        for a, g in enumerate((both[:, :chans], both[:, chans:], third)):
            if n == 0:
                g += dot_nt(strip_taps[a * per : (a + 1) * per], dpre_s)
            wide[a * per : (a + 1) * per, :chans] = g
        for k in range(3):
            at = (3 * n + k) * quarter
            rows = wide[k * quarter : (k + 1) * quarter, :]
            extra = roll(wide[3 * quarter : 4 * quarter, :], chans - k * piece)
            out_ref[at : at + quarter, :] = jnp.where(lane_q < chans, rows, extra)

    start = 6 * quarter
    for j in range(ends // 128):
        at = start + j * chans
        out_ref[at : at + chans, :] = gp[j * 128 : (j + 1) * 128, :].T * inv_npix
    end = start + ends // 128 * chans
    out_ref[end:, :] = jnp.zeros((out_ref.shape[0] - end, 128), F32)


def unpack_kernel(v_ref, gin_ref, gout_ref, gproj_ref):
    chans = gproj_ref.shape[0]
    quarter = 9 * chans // 4
    piece = chans // 3
    for n, ref in enumerate((gin_ref, gout_ref)):
        for k in range(3):
            at = (3 * n + k) * quarter
            ref[k * quarter : (k + 1) * quarter, :] = v_ref[at : at + quarter, :chans]
            ref[3 * quarter :, k * piece : (k + 1) * piece] = v_ref[at : at + quarter, chans:]
    start = 6 * quarter
    for j in range(gproj_ref.shape[1] // 128):
        at = start + j * chans
        gproj_ref[:, j * 128 : (j + 1) * 128] = v_ref[at : at + chans, :]


VMEM = pl.BlockSpec(memory_space=pltpu.VMEM)
ANY = pl.BlockSpec(memory_space=pl.ANY)


def grant(mib):
    return pltpu.CompilerParams(vmem_limit_bytes=mib << 20)


def swap(v, bits):
    n = lax.axis_size("row") * lax.axis_size("col")
    return lax.ppermute(v, ("row", "col"), [(i, i ^ bits[i & 1]) for i in range(n)])


def sum_all(v):
    me = lax.axis_index("row") * lax.axis_size("col") + lax.axis_index("col")
    n = lax.axis_size("row") * lax.axis_size("col")
    bits = [1 << k for k in range(1, n.bit_length() - 1)]
    steps = [(1, 1)]
    for k in range(len(bits)):
        other = k ^ 1 if k ^ 1 < len(bits) else k
        steps.append((bits[k], bits[other]))
    halved, rest = steps[:3], steps[3:]

    def upper(pair):
        return (me & jnp.where(me % 2 == 0, pair[0], pair[1])) != 0

    for pair in halved:
        mine = upper(pair).astype(jnp.int32)
        half = v.shape[0] // 2
        give = lax.dynamic_slice_in_dim(v, (1 - mine) * half, half, 0)
        keep = lax.dynamic_slice_in_dim(v, mine * half, half, 0)
        v = keep + swap(give, pair)
    for pair in rest:
        v = v + swap(v, pair)
    for pair in halved[::-1]:
        got = swap(v, pair)
        top = upper(pair)
        v = jnp.concatenate([jnp.where(top, got, v), jnp.where(top, v, got)], 0)
    return v


def shift(v, axis, by):
    n = lax.axis_size(axis)
    return lax.ppermute(v, axis, [(i, i + by) for i in range(n) if 0 <= i + by < n])


def shards(features, teacher, conv_in, conv_out, projector):
    chans, height, width = features.shape
    ends = teacher.shape[0]
    pixels = height * width
    parts = 6
    x2, up, dn = pl.pallas_call(
        feature_kernel,
        in_specs=[VMEM],
        out_specs=[VMEM] * 3,
        out_shape=[
            jax.ShapeDtypeStruct((chans, pixels), BF16),
            jax.ShapeDtypeStruct((chans, 2 * width), BF16),
            jax.ShapeDtypeStruct((chans, 2 * width), BF16),
        ],
        compiler_params=grant(8),
        name="features",
    )(features)
    bot = shift(up, "row", -1)
    top = shift(dn, "row", 1)
    kernels, proj_t = pl.pallas_call(
        weight_kernel,
        in_specs=[VMEM] * 3,
        out_specs=[VMEM] * 2,
        out_shape=[
            jax.ShapeDtypeStruct((3, chans, 9 * chans), BF16),
            jax.ShapeDtypeStruct((ends, chans), BF16),
        ],
        compiler_params=grant(8),
        name="weights",
    )(conv_in, conv_out, projector)
    ml, mr, own = pl.pallas_call(
        strip_kernel,
        in_specs=[VMEM] * 3,
        out_specs=[VMEM] * 3,
        out_shape=[jax.ShapeDtypeStruct((chans, 128), BF16)] * 3,
        compiler_params=grant(8),
        name="strips",
    )(x2, top, bot)
    rs = shift(ml, "col", -1)
    ls = shift(mr, "col", 1)
    row, col = lax.axis_index("row"), lax.axis_index("col")
    flags = jnp.stack(
        [row > 0, row < lax.axis_size("row") - 1, col > 0, col < lax.axis_size("col") - 1]
    ).astype(jnp.int32)
    npix = pixels * lax.axis_size("row") * lax.axis_size("col")
    total = 2 * 9 * chans * chans // 128 + ends // 128 * chans
    total = -(-total // 64) * 64
    arrays = (kernels, x2, own, ls, rs, top, bot, proj_t, projector, teacher)
    v = pl.pallas_call(
        functools.partial(main_kernel, inv_npix=1.0 / npix, count=len(arrays)),
        in_specs=[pl.BlockSpec(memory_space=pltpu.SMEM)] + [ANY] * len(arrays),
        out_specs=VMEM,
        out_shape=jax.ShapeDtypeStruct((total, 128), F32),
        scratch_shapes=[
            pltpu.VMEM((3 * chans, (height + 4) * width), BF16),
            pltpu.VMEM((3 * chans, (height + 2) * width), BF16),
            pltpu.VMEM((3 * chans, (height + 4) * width), BF16),
            pltpu.VMEM((chans, (height + 2) * width), F32),
            pltpu.VMEM((chans, pixels), BF16),
            pltpu.VMEM((2 * chans, (height + 3) * width), BF16),
            pltpu.VMEM((2 * chans, (height + 1) * width), BF16),
            pltpu.VMEM((9 * chans, 128), F32),
            pltpu.VMEM((ends, chans), F32),
            pltpu.VMEM((ends, pixels), BF16),
            pltpu.SemaphoreType.DMA((len(arrays) - 1 + parts,)),
        ]
        + [pltpu.VMEM(a.shape, a.dtype) for a in arrays],
        compiler_params=grant(48),
        name="block",
    )(flags, *arrays)
    v = sum_all(v)
    gin, gout, gproj = pl.pallas_call(
        unpack_kernel,
        in_specs=[VMEM],
        out_specs=[VMEM] * 3,
        out_shape=[
            jax.ShapeDtypeStruct((9 * chans, chans), F32),
            jax.ShapeDtypeStruct((9 * chans, chans), F32),
            jax.ShapeDtypeStruct((chans, ends), F32),
        ],
        compiler_params=grant(12),
        name="unpack",
    )(v)
    return gin.reshape(9, chans, chans), gout.reshape(9, chans, chans), gproj


def solution(mesh):
    in_specs = (P(None, "row", "col"), P(None, "row", "col"), P(), P(), P())
    out_specs = (P(), P(), P())
    return jax.shard_map(shards, mesh=mesh, in_specs=in_specs, out_specs=out_specs, check_vma=False)
```

```python
import functools

import jax
import jax.numpy as jnp
from jax import lax
from jax.experimental import pallas as pl
from jax.experimental.pallas import tpu as pltpu
from jax.sharding import PartitionSpec as P

F32 = jnp.float32
BF16 = jnp.bfloat16
PITCH = 3
RIGHT = 64


def dot(a, b):
    return jnp.dot(a, b, preferred_element_type=F32)


def dot_nt(a, b):
    return lax.dot_general(a, b, (((1,), (1,)), ((), ())), preferred_element_type=F32)


def split(v):
    hi = v.astype(BF16)
    return hi, (v - hi.astype(F32)).astype(BF16)


def lanes_of(shape):
    return lax.broadcasted_iota(jnp.int32, shape, 1)


def roll(v, by):
    by = by % v.shape[1]
    return v if by == 0 else pltpu.roll(v, by, 1)


def weight_kernel(cin_ref, cout_ref, p_ref, k_ref, pt_ref):
    k_ref[0] = jnp.concatenate([cin_ref[t].T for t in range(9)], 1)
    k_ref[1] = jnp.concatenate([cout_ref[t].T for t in range(9)], 1)
    k_ref[2] = jnp.concatenate([cout_ref[8 - t] for t in range(9)], 1)
    pt_ref[...] = p_ref[...].T


def feature_kernel(x_ref, x2_ref, up_ref, dn_ref):
    height, width = x_ref.shape[1:]
    rows = jnp.swapaxes(x_ref[...], 0, 1)
    for h in range(height):
        x2_ref[:, h * width : (h + 1) * width] = rows[h]
    for h in range(2):
        up_ref[:, h * width : (h + 1) * width] = rows[h]
        dn_ref[:, h * width : (h + 1) * width] = rows[height - 2 + h]


def strip_kernel(x2_ref, top_ref, bot_ref, ml_ref, mr_ref, own_ref):
    chans = x2_ref.shape[0]
    width = top_ref.shape[1] // 2
    height = x2_ref.shape[1] // width
    lane = lanes_of((chans, 128))
    left = right = own = jnp.zeros((chans, 128), F32)
    for r in range(height + 4):
        if r < 2:
            ref, base = top_ref, r * width
        elif r < height + 2:
            ref, base = x2_ref, (r - 2) * width
        else:
            ref, base = bot_ref, (r - height - 2) * width
        first = ref[:, base : base + 128].astype(F32)
        last = ref[:, base + width - 128 : base + width].astype(F32)
        at = r * PITCH
        left = jnp.where((lane >= at + 1) & (lane < at + 3), roll(first, at + 1), left)
        right = jnp.where((lane >= at) & (lane < at + 2), roll(last, at - 126), right)
        own = jnp.where(lane == at + 2, roll(first, at + 2), own)
        own = jnp.where(lane == at + RIGHT, roll(last, at + RIGHT - 127), own)
    ml_ref[...] = left.astype(BF16)
    mr_ref[...] = right.astype(BF16)
    own_ref[...] = own.astype(BF16)


def gelu_and_slope(pre):
    cdf = 0.5 * (1.0 + lax.erf(pre * 0.7071067811865476))
    dens = jnp.exp(-0.5 * pre * pre) * 0.3989422804014327
    return pre * cdf, cdf + pre * dens


def main_kernel(flags, *refs, inv_npix, count):
    hbm, refs = refs[:count], refs[count:]
    out_ref, x3, h3, d3, grad, s2, dpre2, ds2, wide, gp, tr, sem, *refs = refs
    parts = sem.shape[0] - count + 1
    copies = [
        pltpu.make_async_copy(a, b, sem.at[i]) for i, (a, b) in enumerate(zip(hbm[:-1], refs))
    ]
    for c in copies:
        c.start()
    k_ref, x2_ref, own_ref, ls_ref, rs_ref, top_ref, bot_ref, pt_ref, proj_ref, t_ref = refs
    ends = t_ref.shape[0]
    step = ends // parts
    pieces = [
        pltpu.make_async_copy(
            hbm[-1].at[pl.ds(k * step, step)],
            t_ref.at[pl.ds(k * step, step)],
            sem.at[count - 1 + k],
        )
        for k in range(parts)
    ]
    for c in pieces:
        c.start()
    for c in copies[:-2]:
        c.wait()
    chans = x2_ref.shape[0]
    width = top_ref.shape[1] // 2
    height = x2_ref.shape[1] // width
    pixels = height * width
    has_up, has_dn = flags[0].astype(F32), flags[1].astype(F32)
    has_l, has_r = flags[2].astype(F32), flags[3].astype(F32)
    lane = lanes_of((chans, 128))
    kin, kout, kback = k_ref[0], k_ref[1], k_ref[2]

    def taps(v):
        return jnp.concatenate(
            [roll(v, -(a * PITCH + b)) for a in range(3) for b in range(3)], 0
        ).astype(BF16)

    part = lax.rem(lane, RIGHT)
    col = lax.rem(part, PITCH)
    halo_l, halo_r = ls_ref[...].astype(F32), roll(rs_ref[...].astype(F32), RIGHT)
    strip = jnp.where(lane < RIGHT, jnp.where(col < 2, halo_l, 0.0), jnp.where(col > 0, halo_r, 0.0))
    strip = jnp.where(part < (height + 4) * PITCH, strip, 0.0) + own_ref[...].astype(F32)
    strip16 = strip.astype(BF16)
    strip_taps = taps(strip)
    lane1 = lanes_of((1, 128))
    part1 = lax.rem(lane1, RIGHT)
    mask = jnp.where(part1 == 0, has_up, jnp.where(part1 == (height + 1) * PITCH, has_dn, 1.0))
    mask = jnp.where(lane1 < RIGHT, mask * has_l, mask * has_r)
    mask = jnp.where((lax.rem(part1, PITCH) == 0) & (part1 < (height + 2) * PITCH), mask, 0.0)
    hid_s, grad_s = gelu_and_slope(dot(kin, strip_taps))
    hid_s = (hid_s * mask).astype(BF16)
    grad_s = grad_s * mask

    def put(dst, r, seg, rim, at):
        lo, hi = r * width, (r + 1) * width
        ahead = roll(seg, 1)
        first = roll(rim, -at) if rim is not None else jnp.zeros((chans, 128), BF16)
        dst[0:chans, lo : lo + 128] = jnp.where(lane == 0, first, ahead[:, :128])
        dst[0:chans, lo + 128 : hi] = ahead[:, 128:]
        dst[chans : 2 * chans, lo:hi] = seg
        back = roll(seg, -1)
        last = roll(rim, 127 - RIGHT - at) if rim is not None else jnp.zeros((chans, 128), BF16)
        dst[2 * chans :, lo : hi - 128] = back[:, : width - 128]
        dst[2 * chans :, hi - 128 : hi] = jnp.where(lane == 127, last, back[:, width - 128 :])

    def rows3(src, r):
        return jnp.concatenate(
            [src[:, (r + a) * width : (r + a + 1) * width] for a in range(3)], 0
        )

    for r in range(height + 4):
        if r < 2:
            seg = top_ref[:, r * width : (r + 1) * width]
        elif r < height + 2:
            seg = x2_ref[:, (r - 2) * width : (r - 1) * width]
        else:
            seg = bot_ref[:, (r - height - 2) * width : (r - height - 1) * width]
        put(x3, r, seg, strip16, r * PITCH + 1)

    def teach(k):
        pieces[k].wait()
        rows = jnp.swapaxes(t_ref[k * step : (k + 1) * step], 0, 1)
        for h in range(height):
            tr[k * step : (k + 1) * step, h * width : (h + 1) * width] = rows[h]

    for r in range(height + 2):
        hid, slope = gelu_and_slope(dot(kin, rows3(x3, r)))
        if r == 0:
            hid, slope = hid * has_up, slope * has_up
        elif r == height + 1:
            hid, slope = hid * has_dn, slope * has_dn
        grad[:, r * width : (r + 1) * width] = slope
        put(h3, r, hid.astype(BF16), hid_s, r * PITCH)

    for r in range(height):
        span = slice(r * width, (r + 1) * width)
        seg = x2_ref[:, span].astype(F32)
        s2[:, span] = (seg + dot(kout, rows3(h3, r))).astype(BF16)
        if r % 2 == 1 and r < 12:
            teach(r // 2)

    for c in copies[-2:]:
        c.wait()
    proj_t, proj = pt_ref[...], proj_ref[...]
    rim = jnp.zeros((3 * chans, 2 * width), BF16)
    d3[:, : 2 * width] = rim
    d3[:, (height + 2) * width :] = rim
    ds_s = jnp.zeros((chans, 128), F32)
    group = width
    count = pixels // group

    def predict(k):
        return dot(proj_t, s2[:, k * group : (k + 1) * group])

    pred = predict(0)
    for k in range(count):
        span = slice(k * group, (k + 1) * group)
        following = predict(min(k + 1, count - 1))
        dpred = (pred - tr[:, span].astype(F32)).astype(BF16)
        cross = dot_nt(dpred, s2[:, span])
        if k == 0:
            gp[...] = cross
        else:
            gp[...] += cross
        ds_k = (dot(proj, dpred) * inv_npix).astype(BF16)
        pred = following
        for r in range(k * group // width, (k + 1) * group // width):
            at = r * width - k * group
            ds = ds_k[:, at : at + width]
            put(d3, r + 2, ds, None, 0)
            ds2[:chans, r * width : (r + 1) * width] = ds
            ds2[chans:, (r + 1) * width : (r + 2) * width] = ds
            at = (r + 2) * PITCH
            ds32 = ds.astype(F32)
            ds_s = jnp.where(lane == at + 2, roll(ds32[:, :128], at + 2), ds_s)
            ds_s = jnp.where(lane == at + RIGHT, roll(ds32[:, width - 128 :], at + RIGHT - 127), ds_s)

    blank = jnp.zeros((chans, width), BF16)
    for pair, last in ((dpre2, height + 2), (ds2, height)):
        pair[:chans, last * width :] = blank
        pair[chans:, :width] = blank

    for r in range(height + 2):
        span = slice(r * width, (r + 1) * width)
        dpre = (dot(kback, rows3(d3, r)) * grad[:, span]).astype(BF16)
        dpre2[:chans, span] = dpre
        dpre2[chans:, (r + 1) * width : (r + 2) * width] = dpre
    dpre_s = (dot(kback, taps(ds_s)) * grad_s).astype(BF16)

    per = 3 * chans
    quarter = 9 * chans // 4
    piece = chans // 3
    lane_q = lanes_of((quarter, 128))
    for n, (src, pair) in enumerate(((x3, dpre2), (h3, ds2))):
        size = pair.shape[1]
        both = dot_nt(src[:, :size], pair[...])
        third = dot_nt(src[:, 2 * width : width + size], pair[:chans, : size - width])
        for a, g in enumerate((both[:, :chans], both[:, chans:], third)):
            if n == 0:
                g += dot_nt(strip_taps[a * per : (a + 1) * per], dpre_s)
            wide[a * per : (a + 1) * per, :chans] = g
        for k in range(3):
            at = (3 * n + k) * quarter
            rows = wide[k * quarter : (k + 1) * quarter, :]
            extra = roll(wide[3 * quarter : 4 * quarter, :], chans - k * piece)
            out_ref[at : at + quarter, :] = jnp.where(lane_q < chans, rows, extra)

    start = 6 * quarter
    for j in range(ends // 128):
        at = start + j * chans
        out_ref[at : at + chans, :] = gp[j * 128 : (j + 1) * 128, :].T * inv_npix
    end = start + ends // 128 * chans
    out_ref[end:, :] = jnp.zeros((out_ref.shape[0] - end, 128), F32)


def unpack_kernel(v_ref, gin_ref, gout_ref, gproj_ref):
    chans = gproj_ref.shape[0]
    quarter = 9 * chans // 4
    piece = chans // 3
    for n, ref in enumerate((gin_ref, gout_ref)):
        for k in range(3):
            at = (3 * n + k) * quarter
            ref[k * quarter : (k + 1) * quarter, :] = v_ref[at : at + quarter, :chans]
            ref[3 * quarter :, k * piece : (k + 1) * piece] = v_ref[at : at + quarter, chans:]
    start = 6 * quarter
    for j in range(gproj_ref.shape[1] // 128):
        at = start + j * chans
        gproj_ref[:, j * 128 : (j + 1) * 128] = v_ref[at : at + chans, :]


VMEM = pl.BlockSpec(memory_space=pltpu.VMEM)
ANY = pl.BlockSpec(memory_space=pl.ANY)


def grant(mib):
    return pltpu.CompilerParams(vmem_limit_bytes=mib << 20)


def swap(v, bits, other=None):
    n = lax.axis_size("row") * lax.axis_size("col")
    pick = (bits, bits if other is None else other)
    return lax.ppermute(v, ("row", "col"), [(i, i ^ pick[i & 1]) for i in range(n)])


def sum_all(v):
    me = lax.axis_index("row") * lax.axis_size("col") + lax.axis_index("col")
    n = lax.axis_size("row") * lax.axis_size("col")

    def rows_of(v, parts, k):
        size = v.shape[0] // parts
        return lax.dynamic_slice_in_dim(v, k * size, size, 0)

    core, chip = me & 1, (me >> 1) & 3
    v = rows_of(v, 2, core) + swap(rows_of(v, 2, 1 - core), 1)
    got = [swap(rows_of(v, 4, chip ^ k), k << 1) for k in (1, 2, 3)]
    v = ((rows_of(v, 4, chip) + got[0]) + got[1]) + got[2]
    rest = [1 << k for k in range(3, n.bit_length() - 1)]
    for bits, other in zip(rest, rest[::-1]):
        v = v + swap(v, bits, other)
    got = [v] + [swap(v, k << 1) for k in (1, 2, 3)]
    pieces = []
    for q in range(4):
        piece = got[3]
        for k in range(3):
            piece = jnp.where(chip ^ q == k, got[k], piece)
        pieces.append(piece)
    v = jnp.concatenate(pieces, 0)
    other = swap(v, 1)
    return jnp.concatenate([jnp.where(core == 0, v, other), jnp.where(core == 0, other, v)], 0)


def shift(v, axis, by):
    n = lax.axis_size(axis)
    return lax.ppermute(v, axis, [(i, i + by) for i in range(n) if 0 <= i + by < n])


def shards(features, teacher, conv_in, conv_out, projector):
    chans, height, width = features.shape
    ends = teacher.shape[0]
    pixels = height * width
    parts = 6
    x2, up, dn = pl.pallas_call(
        feature_kernel,
        in_specs=[VMEM],
        out_specs=[VMEM] * 3,
        out_shape=[
            jax.ShapeDtypeStruct((chans, pixels), BF16),
            jax.ShapeDtypeStruct((chans, 2 * width), BF16),
            jax.ShapeDtypeStruct((chans, 2 * width), BF16),
        ],
        compiler_params=grant(8),
        name="features",
    )(features)
    bot = shift(up, "row", -1)
    top = shift(dn, "row", 1)
    kernels, proj_t = pl.pallas_call(
        weight_kernel,
        in_specs=[VMEM] * 3,
        out_specs=[VMEM] * 2,
        out_shape=[
            jax.ShapeDtypeStruct((3, chans, 9 * chans), BF16),
            jax.ShapeDtypeStruct((ends, chans), BF16),
        ],
        compiler_params=grant(8),
        name="weights",
    )(conv_in, conv_out, projector)
    ml, mr, own = pl.pallas_call(
        strip_kernel,
        in_specs=[VMEM] * 3,
        out_specs=[VMEM] * 3,
        out_shape=[jax.ShapeDtypeStruct((chans, 128), BF16)] * 3,
        compiler_params=grant(8),
        name="strips",
    )(x2, top, bot)
    rs = shift(ml, "col", -1)
    ls = shift(mr, "col", 1)
    row, col = lax.axis_index("row"), lax.axis_index("col")
    flags = jnp.stack(
        [row > 0, row < lax.axis_size("row") - 1, col > 0, col < lax.axis_size("col") - 1]
    ).astype(jnp.int32)
    npix = pixels * lax.axis_size("row") * lax.axis_size("col")
    total = 2 * 9 * chans * chans // 128 + ends // 128 * chans
    total = -(-total // 64) * 64
    arrays = (kernels, x2, own, ls, rs, top, bot, proj_t, projector, teacher)
    v = pl.pallas_call(
        functools.partial(main_kernel, inv_npix=1.0 / npix, count=len(arrays)),
        in_specs=[pl.BlockSpec(memory_space=pltpu.SMEM)] + [ANY] * len(arrays),
        out_specs=VMEM,
        out_shape=jax.ShapeDtypeStruct((total, 128), F32),
        scratch_shapes=[
            pltpu.VMEM((3 * chans, (height + 4) * width), BF16),
            pltpu.VMEM((3 * chans, (height + 2) * width), BF16),
            pltpu.VMEM((3 * chans, (height + 4) * width), BF16),
            pltpu.VMEM((chans, (height + 2) * width), F32),
            pltpu.VMEM((chans, pixels), BF16),
            pltpu.VMEM((2 * chans, (height + 3) * width), BF16),
            pltpu.VMEM((2 * chans, (height + 1) * width), BF16),
            pltpu.VMEM((9 * chans, 128), F32),
            pltpu.VMEM((ends, chans), F32),
            pltpu.VMEM((ends, pixels), BF16),
            pltpu.SemaphoreType.DMA((len(arrays) - 1 + parts,)),
        ]
        + [pltpu.VMEM(a.shape, a.dtype) for a in arrays],
        compiler_params=grant(48),
        name="block",
    )(flags, *arrays)
    v = sum_all(v)
    gin, gout, gproj = pl.pallas_call(
        unpack_kernel,
        in_specs=[VMEM],
        out_specs=[VMEM] * 3,
        out_shape=[
            jax.ShapeDtypeStruct((9 * chans, chans), F32),
            jax.ShapeDtypeStruct((9 * chans, chans), F32),
            jax.ShapeDtypeStruct((chans, ends), F32),
        ],
        compiler_params=grant(12),
        name="unpack",
    )(v)
    return gin.reshape(9, chans, chans), gout.reshape(9, chans, chans), gproj


def solution(mesh):
    in_specs = (P(None, "row", "col"), P(None, "row", "col"), P(), P(), P())
    out_specs = (P(), P(), P())
    return jax.shard_map(shards, mesh=mesh, in_specs=in_specs, out_specs=out_specs, check_vma=False)
```

```python
import functools

import jax
import jax.numpy as jnp
from jax import lax
from jax.experimental import pallas as pl
from jax.experimental.pallas import tpu as pltpu
from jax.sharding import PartitionSpec as P

F32 = jnp.float32
BF16 = jnp.bfloat16
PITCH = 3
RIGHT = 64


def dot(a, b):
    return jnp.dot(a, b, preferred_element_type=F32)


def dot_nt(a, b):
    return lax.dot_general(a, b, (((1,), (1,)), ((), ())), preferred_element_type=F32)


def split(v):
    hi = v.astype(BF16)
    return hi, (v - hi.astype(F32)).astype(BF16)


def lanes_of(shape):
    return lax.broadcasted_iota(jnp.int32, shape, 1)


def roll(v, by):
    by = by % v.shape[1]
    return v if by == 0 else pltpu.roll(v, by, 1)


def weight_kernel(cin_ref, cout_ref, p_ref, k_ref, pt_ref):
    k_ref[0] = jnp.concatenate([cin_ref[t].T for t in range(9)], 1)
    k_ref[1] = jnp.concatenate([cout_ref[t].T for t in range(9)], 1)
    k_ref[2] = jnp.concatenate([cout_ref[8 - t] for t in range(9)], 1)
    pt_ref[...] = p_ref[...].T


def feature_kernel(x_ref, x2_ref, up_ref, dn_ref):
    height, width = x_ref.shape[1:]
    rows = jnp.swapaxes(x_ref[...], 0, 1)
    for h in range(height):
        x2_ref[:, h * width : (h + 1) * width] = rows[h]
    for h in range(2):
        up_ref[:, h * width : (h + 1) * width] = rows[h]
        dn_ref[:, h * width : (h + 1) * width] = rows[height - 2 + h]


def strip_row(left, right, own, first, last, at, lane):
    left = jnp.where((lane >= at + 1) & (lane < at + 3), roll(first, at + 1), left)
    right = jnp.where((lane >= at) & (lane < at + 2), roll(last, at - 126), right)
    own = jnp.where(lane == at + 2, roll(first, at + 2), own)
    own = jnp.where(lane == at + RIGHT, roll(last, at + RIGHT - 127), own)
    return left, right, own


def own_kernel(x2_ref, part_ref, *, width):
    chans = x2_ref.shape[0]
    lane = lanes_of((chans, 128))
    strips = (jnp.zeros((chans, 128), BF16),) * 3
    for r in range(x2_ref.shape[1] // width):
        first = x2_ref[:, r * width : r * width + 128]
        last = x2_ref[:, (r + 1) * width - 128 : (r + 1) * width]
        strips = strip_row(*strips, first, last, (r + 2) * PITCH, lane)
    for k in range(3):
        part_ref[k] = strips[k]


def strip_kernel(part_ref, top_ref, bot_ref, ml_ref, mr_ref, own_ref, *, height):
    width = top_ref.shape[1] // 2
    lane = lanes_of((part_ref.shape[1], 128))
    strips = (part_ref[0], part_ref[1], part_ref[2])
    for r in range(2):
        for ref, at in ((top_ref, r * PITCH), (bot_ref, (height + 2 + r) * PITCH)):
            first = ref[:, r * width : r * width + 128]
            last = ref[:, (r + 1) * width - 128 : (r + 1) * width]
            strips = strip_row(*strips, first, last, at, lane)
    for ref, v in zip((ml_ref, mr_ref, own_ref), strips):
        ref[...] = v


def gelu_and_slope(pre):
    cdf = 0.5 * (1.0 + lax.erf(pre * 0.7071067811865476))
    dens = jnp.exp(-0.5 * pre * pre) * 0.3989422804014327
    return pre * cdf, cdf + pre * dens


def main_kernel(flags, *refs, inv_npix, count):
    hbm, refs = refs[:count], refs[count:]
    out_ref, x3, h3, d3, grad, s2, dpre2, ds2, wide, gp, tr, sem, *refs = refs
    parts = sem.shape[0] - count + 1
    copies = [
        pltpu.make_async_copy(a, b, sem.at[i]) for i, (a, b) in enumerate(zip(hbm[:-1], refs))
    ]
    for c in copies:
        c.start()
    k_ref, x2_ref, own_ref, ls_ref, rs_ref, top_ref, bot_ref, pt_ref, proj_ref, t_ref = refs
    ends = t_ref.shape[0]
    step = ends // parts
    pieces = [
        pltpu.make_async_copy(
            hbm[-1].at[pl.ds(k * step, step)],
            t_ref.at[pl.ds(k * step, step)],
            sem.at[count - 1 + k],
        )
        for k in range(parts)
    ]
    for c in pieces:
        c.start()
    for c in copies[:-2]:
        c.wait()
    chans = x2_ref.shape[0]
    width = top_ref.shape[1] // 2
    height = x2_ref.shape[1] // width
    pixels = height * width
    has_up, has_dn = flags[0].astype(F32), flags[1].astype(F32)
    has_l, has_r = flags[2].astype(F32), flags[3].astype(F32)
    lane = lanes_of((chans, 128))
    kin, kout, kback = k_ref[0], k_ref[1], k_ref[2]

    def taps(v):
        return jnp.concatenate(
            [roll(v, -(a * PITCH + b)) for a in range(3) for b in range(3)], 0
        ).astype(BF16)

    part = lax.rem(lane, RIGHT)
    col = lax.rem(part, PITCH)
    halo_l, halo_r = ls_ref[...].astype(F32), roll(rs_ref[...].astype(F32), RIGHT)
    strip = jnp.where(lane < RIGHT, jnp.where(col < 2, halo_l, 0.0), jnp.where(col > 0, halo_r, 0.0))
    strip = jnp.where(part < (height + 4) * PITCH, strip, 0.0) + own_ref[...].astype(F32)
    strip16 = strip.astype(BF16)
    strip_taps = taps(strip)
    lane1 = lanes_of((1, 128))
    part1 = lax.rem(lane1, RIGHT)
    mask = jnp.where(part1 == 0, has_up, jnp.where(part1 == (height + 1) * PITCH, has_dn, 1.0))
    mask = jnp.where(lane1 < RIGHT, mask * has_l, mask * has_r)
    mask = jnp.where((lax.rem(part1, PITCH) == 0) & (part1 < (height + 2) * PITCH), mask, 0.0)
    hid_s, grad_s = gelu_and_slope(dot(kin, strip_taps))
    hid_s = (hid_s * mask).astype(BF16)
    grad_s = grad_s * mask

    def put(dst, r, seg, rim, at):
        lo, hi = r * width, (r + 1) * width
        ahead = roll(seg, 1)
        first = roll(rim, -at) if rim is not None else jnp.zeros((chans, 128), BF16)
        dst[0:chans, lo : lo + 128] = jnp.where(lane == 0, first, ahead[:, :128])
        dst[0:chans, lo + 128 : hi] = ahead[:, 128:]
        dst[chans : 2 * chans, lo:hi] = seg
        back = roll(seg, -1)
        last = roll(rim, 127 - RIGHT - at) if rim is not None else jnp.zeros((chans, 128), BF16)
        dst[2 * chans :, lo : hi - 128] = back[:, : width - 128]
        dst[2 * chans :, hi - 128 : hi] = jnp.where(lane == 127, last, back[:, width - 128 :])

    def rows3(src, r):
        return jnp.concatenate(
            [src[:, (r + a) * width : (r + a + 1) * width] for a in range(3)], 0
        )

    for r in range(height + 4):
        if r < 2:
            seg = top_ref[:, r * width : (r + 1) * width]
        elif r < height + 2:
            seg = x2_ref[:, (r - 2) * width : (r - 1) * width]
        else:
            seg = bot_ref[:, (r - height - 2) * width : (r - height - 1) * width]
        put(x3, r, seg, strip16, r * PITCH + 1)

    def teach(k):
        pieces[k].wait()
        rows = jnp.swapaxes(t_ref[k * step : (k + 1) * step], 0, 1)
        for h in range(height):
            tr[k * step : (k + 1) * step, h * width : (h + 1) * width] = rows[h]

    for r in range(height + 2):
        hid, slope = gelu_and_slope(dot(kin, rows3(x3, r)))
        if r == 0:
            hid, slope = hid * has_up, slope * has_up
        elif r == height + 1:
            hid, slope = hid * has_dn, slope * has_dn
        grad[:, r * width : (r + 1) * width] = slope
        put(h3, r, hid.astype(BF16), hid_s, r * PITCH)

    for r in range(height):
        span = slice(r * width, (r + 1) * width)
        seg = x2_ref[:, span].astype(F32)
        s2[:, span] = (seg + dot(kout, rows3(h3, r))).astype(BF16)
        if r % 2 == 1 and r < 12:
            teach(r // 2)

    for c in copies[-2:]:
        c.wait()
    proj_t, proj = pt_ref[...], proj_ref[...]
    rim = jnp.zeros((3 * chans, 2 * width), BF16)
    d3[:, : 2 * width] = rim
    d3[:, (height + 2) * width :] = rim
    ds_s = jnp.zeros((chans, 128), F32)
    group = width
    count = pixels // group

    def predict(k):
        return dot(proj_t, s2[:, k * group : (k + 1) * group])

    pred = predict(0)
    for k in range(count):
        span = slice(k * group, (k + 1) * group)
        following = predict(min(k + 1, count - 1))
        dpred = (pred - tr[:, span].astype(F32)).astype(BF16)
        cross = dot_nt(dpred, s2[:, span])
        if k == 0:
            gp[...] = cross
        else:
            gp[...] += cross
        ds_k = (dot(proj, dpred) * inv_npix).astype(BF16)
        pred = following
        for r in range(k * group // width, (k + 1) * group // width):
            at = r * width - k * group
            ds = ds_k[:, at : at + width]
            put(d3, r + 2, ds, None, 0)
            ds2[:chans, r * width : (r + 1) * width] = ds
            ds2[chans:, (r + 1) * width : (r + 2) * width] = ds
            at = (r + 2) * PITCH
            ds32 = ds.astype(F32)
            ds_s = jnp.where(lane == at + 2, roll(ds32[:, :128], at + 2), ds_s)
            ds_s = jnp.where(lane == at + RIGHT, roll(ds32[:, width - 128 :], at + RIGHT - 127), ds_s)

    blank = jnp.zeros((chans, width), BF16)
    for pair, last in ((dpre2, height + 2), (ds2, height)):
        pair[:chans, last * width :] = blank
        pair[chans:, :width] = blank

    for r in range(height + 2):
        span = slice(r * width, (r + 1) * width)
        dpre = (dot(kback, rows3(d3, r)) * grad[:, span]).astype(BF16)
        dpre2[:chans, span] = dpre
        dpre2[chans:, (r + 1) * width : (r + 2) * width] = dpre
    dpre_s = (dot(kback, taps(ds_s)) * grad_s).astype(BF16)

    per = 3 * chans
    quarter = 9 * chans // 4
    piece = chans // 3
    lane_q = lanes_of((quarter, 128))
    for n, (src, pair) in enumerate(((x3, dpre2), (h3, ds2))):
        size = pair.shape[1]
        both = dot_nt(src[:, :size], pair[...])
        third = dot_nt(src[:, 2 * width : width + size], pair[:chans, : size - width])
        for a, g in enumerate((both[:, :chans], both[:, chans:], third)):
            if n == 0:
                g += dot_nt(strip_taps[a * per : (a + 1) * per], dpre_s)
            wide[a * per : (a + 1) * per, :chans] = g
        for k in range(3):
            at = (3 * n + k) * quarter
            rows = wide[k * quarter : (k + 1) * quarter, :]
            extra = roll(wide[3 * quarter : 4 * quarter, :], chans - k * piece)
            out_ref[at : at + quarter, :] = jnp.where(lane_q < chans, rows, extra)

    start = 6 * quarter
    for j in range(ends // 128):
        at = start + j * chans
        out_ref[at : at + chans, :] = gp[j * 128 : (j + 1) * 128, :].T * inv_npix
    end = start + ends // 128 * chans
    out_ref[end:, :] = jnp.zeros((out_ref.shape[0] - end, 128), F32)


def unpack_kernel(v_ref, gin_ref, gout_ref, gproj_ref):
    chans = gproj_ref.shape[0]
    quarter = 9 * chans // 4
    piece = chans // 3
    for n, ref in enumerate((gin_ref, gout_ref)):
        for k in range(3):
            at = (3 * n + k) * quarter
            ref[k * quarter : (k + 1) * quarter, :] = v_ref[at : at + quarter, :chans]
            ref[3 * quarter :, k * piece : (k + 1) * piece] = v_ref[at : at + quarter, chans:]
    start = 6 * quarter
    for j in range(gproj_ref.shape[1] // 128):
        at = start + j * chans
        gproj_ref[:, j * 128 : (j + 1) * 128] = v_ref[at : at + chans, :]


VMEM = pl.BlockSpec(memory_space=pltpu.VMEM)
ANY = pl.BlockSpec(memory_space=pl.ANY)


def grant(mib):
    return pltpu.CompilerParams(vmem_limit_bytes=mib << 20)


def swap(v, bits, other=None):
    n = lax.axis_size("row") * lax.axis_size("col")
    pick = (bits, bits if other is None else other)
    return lax.ppermute(v, ("row", "col"), [(i, i ^ pick[i & 1]) for i in range(n)])


def sum_all(v):
    me = lax.axis_index("row") * lax.axis_size("col") + lax.axis_index("col")
    n = lax.axis_size("row") * lax.axis_size("col")

    def rows_of(v, parts, k):
        size = v.shape[0] // parts
        return lax.dynamic_slice_in_dim(v, k * size, size, 0)

    core, chip = me & 1, (me >> 1) & 3
    v = rows_of(v, 2, core) + swap(rows_of(v, 2, 1 - core), 1)
    got = [swap(rows_of(v, 4, chip ^ k), k << 1) for k in (1, 2, 3)]
    v = ((rows_of(v, 4, chip) + got[0]) + got[1]) + got[2]
    rest = [1 << k for k in range(3, n.bit_length() - 1)]
    for bits, other in zip(rest, rest[::-1]):
        v = v + swap(v, bits, other)
    got = [v] + [swap(v, k << 1) for k in (1, 2, 3)]
    pieces = []
    for q in range(4):
        piece = got[3]
        for k in range(3):
            piece = jnp.where(chip ^ q == k, got[k], piece)
        pieces.append(piece)
    v = jnp.concatenate(pieces, 0)
    other = swap(v, 1)
    return jnp.concatenate([jnp.where(core == 0, v, other), jnp.where(core == 0, other, v)], 0)


def shift(v, axis, by):
    n = lax.axis_size(axis)
    return lax.ppermute(v, axis, [(i, i + by) for i in range(n) if 0 <= i + by < n])


def shards(features, teacher, conv_in, conv_out, projector):
    chans, height, width = features.shape
    ends = teacher.shape[0]
    pixels = height * width
    parts = 6
    x2, up, dn = pl.pallas_call(
        feature_kernel,
        in_specs=[VMEM],
        out_specs=[VMEM] * 3,
        out_shape=[
            jax.ShapeDtypeStruct((chans, pixels), BF16),
            jax.ShapeDtypeStruct((chans, 2 * width), BF16),
            jax.ShapeDtypeStruct((chans, 2 * width), BF16),
        ],
        compiler_params=grant(8),
        name="features",
    )(features)
    bot = shift(up, "row", -1)
    top = shift(dn, "row", 1)
    kernels, proj_t = pl.pallas_call(
        weight_kernel,
        in_specs=[VMEM] * 3,
        out_specs=[VMEM] * 2,
        out_shape=[
            jax.ShapeDtypeStruct((3, chans, 9 * chans), BF16),
            jax.ShapeDtypeStruct((ends, chans), BF16),
        ],
        compiler_params=grant(8),
        name="weights",
    )(conv_in, conv_out, projector)
    part = pl.pallas_call(
        functools.partial(own_kernel, width=width),
        in_specs=[VMEM],
        out_specs=VMEM,
        out_shape=jax.ShapeDtypeStruct((3, chans, 128), BF16),
        compiler_params=grant(8),
        name="own",
    )(x2)
    ml, mr, own = pl.pallas_call(
        functools.partial(strip_kernel, height=height),
        in_specs=[VMEM] * 3,
        out_specs=[VMEM] * 3,
        out_shape=[jax.ShapeDtypeStruct((chans, 128), BF16)] * 3,
        compiler_params=grant(8),
        name="strips",
    )(part, top, bot)
    rs = shift(ml, "col", -1)
    ls = shift(mr, "col", 1)
    row, col = lax.axis_index("row"), lax.axis_index("col")
    flags = jnp.stack(
        [row > 0, row < lax.axis_size("row") - 1, col > 0, col < lax.axis_size("col") - 1]
    ).astype(jnp.int32)
    npix = pixels * lax.axis_size("row") * lax.axis_size("col")
    total = 2 * 9 * chans * chans // 128 + ends // 128 * chans
    total = -(-total // 64) * 64
    arrays = (kernels, x2, own, ls, rs, top, bot, proj_t, projector, teacher)
    v = pl.pallas_call(
        functools.partial(main_kernel, inv_npix=1.0 / npix, count=len(arrays)),
        in_specs=[pl.BlockSpec(memory_space=pltpu.SMEM)] + [ANY] * len(arrays),
        out_specs=VMEM,
        out_shape=jax.ShapeDtypeStruct((total, 128), F32),
        scratch_shapes=[
            pltpu.VMEM((3 * chans, (height + 4) * width), BF16),
            pltpu.VMEM((3 * chans, (height + 2) * width), BF16),
            pltpu.VMEM((3 * chans, (height + 4) * width), BF16),
            pltpu.VMEM((chans, (height + 2) * width), F32),
            pltpu.VMEM((chans, pixels), BF16),
            pltpu.VMEM((2 * chans, (height + 3) * width), BF16),
            pltpu.VMEM((2 * chans, (height + 1) * width), BF16),
            pltpu.VMEM((9 * chans, 128), F32),
            pltpu.VMEM((ends, chans), F32),
            pltpu.VMEM((ends, pixels), BF16),
            pltpu.SemaphoreType.DMA((len(arrays) - 1 + parts,)),
        ]
        + [pltpu.VMEM(a.shape, a.dtype) for a in arrays],
        compiler_params=grant(48),
        name="block",
    )(flags, *arrays)
    v = sum_all(v)
    gin, gout, gproj = pl.pallas_call(
        unpack_kernel,
        in_specs=[VMEM],
        out_specs=[VMEM] * 3,
        out_shape=[
            jax.ShapeDtypeStruct((9 * chans, chans), F32),
            jax.ShapeDtypeStruct((9 * chans, chans), F32),
            jax.ShapeDtypeStruct((chans, ends), F32),
        ],
        compiler_params=grant(12),
        name="unpack",
    )(v)
    return gin.reshape(9, chans, chans), gout.reshape(9, chans, chans), gproj


def solution(mesh):
    in_specs = (P(None, "row", "col"), P(None, "row", "col"), P(), P(), P())
    out_specs = (P(), P(), P())
    return jax.shard_map(shards, mesh=mesh, in_specs=in_specs, out_specs=out_specs, check_vma=False)
```
